128 devices in a mesh: tm: 32 (over y, x, core), state: 4 (over z).
Axes of the slice: x: 4, y: 4, z: 4, core: 2. Of those that a mesh axis runs over, the one named last changes fastest.
Arguments:
- dynamics: float32 [512, 49152], P('tm', 'state'), may hold values from -0.05 to 1.05, as said below
- band: int32 [512, 4, 2], P('tm', 'state'), may hold values from 0 to 1
- observed: float32 [512, 256], P('tm', 'state'), may hold values from -60 to 60
- obs_mask: int32 [512, 256], P('tm', 'state'), may hold values 0 or 1
- filter_gain: float32 [512, 256], P('tm', 'state'), may hold values from 0.0005 to 0.02
- smooth_gain: float32 [512, 256], P('tm', 'state'), may hold values from 0.97 to 0.9995
Outputs:
- filtered: float32 [512, 256], P('tm', 'state')
- smoothed: float32 [512, 256], P('tm', 'state')
The draws below stay inside these ranges and needn't reach their ends.
Inputs may be any that keep to these rules, and one draw needn't show every extreme that they name: `dynamics`: entries r * 3 * 64 to (r + 1) * 3 * 64 - 1 of a step hold row r's couplings to the block before, its own block and the block after; entries that would reach outside the state are never used.
All inputs are finite; a program needn't handle non-finite values. No bound on the sum of `obs_mask` on one device may be relied on, other than what follows from the above.
Results may differ from the reference program's by a relative error of at most 0.0003.
Values sent between devices are 32-bit elements; how exact they have to be, the bound alone decides.
No kernel may reach another device: no remote copies, remote signals or barrier semaphores. Data moves between devices by JAX's collectives and lax.ppermute only.
A program may use at most 64 MiB of HBM per device.

```python
import math
import jax
import jax.numpy as jnp
from jax import lax

STATE = 256
BLOCK = 64
NBLK = 4
TSTEPS = 512


def draw_dynamics(key, part):
    key = jax.random.fold_in(key, 7)
    key_noise, key_rate, key_rough = jax.random.split(key, 3)
    sigma = 0.06 / math.sqrt(3 * BLOCK)
    noise = jnp.clip(jax.random.normal(key_noise, (TSTEPS, STATE, 3 * BLOCK), jnp.float32), -4.0, 4.0) * sigma
    rate = jnp.exp(jax.random.uniform(key_rate, (1, STATE, 1), jnp.float32, math.log(0.0001), math.log(0.1)))
    rough = jax.random.uniform(key_rough, (TSTEPS, STATE, 1), jnp.float32, 0.5, 1.5)
    row_pos = jax.lax.broadcasted_iota(jnp.int32, (1, STATE, 3 * BLOCK), 1) % BLOCK
    col_pos = jax.lax.broadcasted_iota(jnp.int32, (1, STATE, 3 * BLOCK), 2)
    diagonal = (col_pos == row_pos + BLOCK).astype(jnp.float32)
    result = noise + diagonal * jnp.exp(-rate * rough)
    return result.reshape(TSTEPS, STATE * 3 * BLOCK)


def set_ends(drawn, own_key, low, top_value):
    spot = [jax.random.randint(jax.random.fold_in(own_key, axis), (), 0, length) for axis, length in enumerate(drawn.shape)]
    longest = drawn.shape.index(max(drawn.shape))
    next_to = spot[:longest] + [(spot[longest] + 1) % drawn.shape[longest]] + spot[longest + 1:]
    return drawn.at[tuple(spot)].set(low).at[tuple(next_to)].set(top_value)


def shard_levels(stream_key, dims, cuts, low, largest):
    def one(position, shards_of):
        draws = jax.random.uniform(jax.random.fold_in(jax.random.fold_in(stream_key, 6), position), (shards_of,), jnp.float32, low / len(cuts), largest / len(cuts))
        return jnp.repeat(jnp.exp(draws), dims[position] // shards_of).reshape((-1,) + (1,) * (len(dims) - position - 1))

    factor_of = one(*cuts[0])
    for cut in cuts[1:]:
        factor_of = factor_of * one(*cut)
    return factor_of


def bell_draw(key, shape, width, reach, shards=(), dtype=jnp.bfloat16):
    entries = jax.random.normal(key, shape, jnp.float32) * width
    if len(shards) > 0:
        entries = shard_levels(key, shape, shards, -0.22, 0.18) * entries
    return jnp.clip(entries, min=-reach, max=reach).astype(dtype)


def setup_inputs(seed: int = 0) -> dict:
    arg_keys = jax.random.split(jax.random.key(seed), 7)
    return {
        "dynamics": draw_dynamics(jax.random.fold_in(arg_keys[6], 71), 0),
        "band": set_ends(jax.random.randint(arg_keys[1], (TSTEPS, NBLK, 2), 0, 2), jax.random.fold_in(arg_keys[1], 1), 0, 1).astype(jnp.int32),
        "observed": bell_draw(arg_keys[2], (TSTEPS, STATE), 10.0, 60.0, ((0, 32), (1, 4)), jnp.float32),
        "obs_mask": set_ends((jax.random.randint(arg_keys[3], (TSTEPS, STATE), 0, 2) < 1).astype(jnp.int32), jax.random.fold_in(arg_keys[3], 1), 0, 1),
        "filter_gain": jnp.clip(jnp.exp(math.log(0.02) - 3.6888794 * jax.random.uniform(arg_keys[4], (TSTEPS, STATE), jnp.float32) ** shard_levels(arg_keys[4], (TSTEPS, STATE), ((0, 32), (1, 4)), -0.2, 0.2)), 0.0005, 0.02),
        "smooth_gain": jnp.clip(jnp.exp(math.log(0.9995) - 0.02995903 * jax.random.uniform(arg_keys[5], (TSTEPS, STATE), jnp.float32) ** shard_levels(arg_keys[5], (TSTEPS, STATE), ((0, 32), (1, 4)), -0.2, 0.2)), 0.97, 0.9995),
    }


highest = lax.Precision.HIGHEST


def neighbours(matrix, blocks):
    total = matrix.shape[-2]
    rows = total // blocks
    leading = matrix.shape[:-2]
    padded = jnp.pad(matrix, [(0, 0)] * len(leading) + [(rows, rows), (0, 0)])
    shifted = [padded[..., offset * rows:offset * rows + total, :].reshape(leading + (blocks, rows, matrix.shape[-1])) for offset in range(3)]
    return jnp.concatenate(shifted, axis=-2)


def band_apply(panels, matrix):
    gathered = neighbours(matrix, panels.shape[-3])
    result = jnp.einsum("...ibc,...icw->...ibw", panels, gathered, precision=highest)
    return result.reshape(matrix.shape)


def band_transpose(panels, matrix):
    blocks = panels.shape[-3]
    rows = panels.shape[-2]
    leading = matrix.shape[:-2]
    split_rows = matrix.reshape(leading + (blocks, rows, matrix.shape[-1]))
    contrib = jnp.einsum("...ibc,...ibw->...icw", panels, split_rows, precision=highest)
    summed = 0.0
    for offset in range(3):
        piece = contrib[..., offset * rows:(offset + 1) * rows, :]
        summed = summed + jnp.pad(piece, [(0, 0)] * len(leading) + [(offset, 2 - offset), (0, 0), (0, 0)])
    return summed[..., 1:blocks + 1, :, :].reshape(matrix.shape)


def reference(dynamics, band, observed, obs_mask, filter_gain, smooth_gain):
    steps, state_dim = observed.shape
    blocks = state_dim // BLOCK
    lower = band[:, :, 0].astype(jnp.float32)[:, :, None, None]
    upper = band[:, :, 1].astype(jnp.float32)[:, :, None, None]
    panels = dynamics.reshape(steps, blocks, BLOCK, 3 * BLOCK)
    panels = jnp.concatenate([panels[..., :BLOCK] * lower, panels[..., BLOCK:2 * BLOCK], panels[..., 2 * BLOCK:] * upper], axis=-1)
    weight = obs_mask.astype(jnp.float32) * filter_gain
    drive = weight * observed

    def forward(mean, inputs):
        step_panels, step_weight, step_drive = inputs
        mean = (1.0 - step_weight) * band_apply(step_panels, mean[:, None])[:, 0] + step_drive
        return mean, mean

    start = jnp.zeros((state_dim,), jnp.float32)
    final_mean, filtered = lax.scan(forward, start, (panels, weight, drive))
    following = jnp.concatenate([panels[1:], jnp.zeros_like(panels[:1])], axis=0)

    def backward(later, inputs):
        step_panels, step_gain, mean = inputs
        gap = later - band_apply(step_panels, mean[:, None])[:, 0]
        smooth = mean + step_gain * band_transpose(step_panels, gap[:, None])[:, 0]
        return smooth, smooth

    first_mean, smoothed = lax.scan(backward, start, (following, smooth_gain, filtered), reverse=True)
    return filtered, smoothed
```

```python
import jax
import jax.numpy as jnp
from jax import lax
from jax.experimental import pallas as pl
from jax.experimental.pallas import tpu as pltpu
from jax.sharding import PartitionSpec as P

BLOCK = 64
STATE = 256
BLOCKS = 4
STEPS = 16
AUG = STATE + 8
MIB = 1 << 20

f32 = jnp.float32
bf16 = jnp.bfloat16


def split(a):
    hi = a.astype(bf16)
    return hi, (a - hi.astype(f32)).astype(bf16)


def dot_nn(a, b):
    return lax.dot_general(a, b, (((1,), (0,)), ((), ())), preferred_element_type=f32)


def dot_nt(a, b):
    return lax.dot_general(a, b, (((1,), (1,)), ((), ())), preferred_element_type=f32)


def three(dot, a, b):
    ahi, alo = a
    bhi, blo = b
    return dot(ahi, bhi) + (dot(alo, bhi) + dot(ahi, blo))


def mul_nn(a, b):
    return three(dot_nn, split(a), split(b))


def mul_nt(a, b):
    return three(dot_nt, split(a), split(b))


def first_row(row):
    spread = jnp.broadcast_to(row, (8, row.shape[1]))
    return jnp.where(lax.broadcasted_iota(jnp.int32, spread.shape, 0) == 0, spread, 0.0)


def identity_matrix():
    rows = lax.broadcasted_iota(jnp.int32, (STATE, STATE), 0)
    cols = lax.broadcasted_iota(jnp.int32, (STATE, STATE), 1)
    return jnp.where(rows == cols, 1.0, 0.0).astype(f32)


def call(kernel, outs, args, scratch=(), limit=40, flops=0):
    vmem = pl.BlockSpec(memory_space=pltpu.VMEM)
    smem = pl.BlockSpec(memory_space=pltpu.SMEM)
    moved = sum(a.size * a.dtype.itemsize for a in args) + sum(
        o.size * o.dtype.itemsize for o in outs
    )
    return pl.pallas_call(
        kernel,
        out_shape=outs,
        in_specs=[smem if a.size < 8 else vmem for a in args],
        out_specs=[vmem] * len(outs),
        scratch_shapes=list(scratch),
        compiler_params=pltpu.CompilerParams(vmem_limit_bytes=limit * MIB),
        cost_estimate=pl.CostEstimate(flops=flops, bytes_accessed=moved, transcendentals=0),
    )(*args)


def arr(*shape, dtype=f32):
    return jax.ShapeDtypeStruct(shape, dtype)


NA = BLOCK * STEPS
NB = NA // 2
PACKED = NA + NB + 2 * STEPS


def pack_kernel(dyn_ref, lower_ref, upper_ref, obs_ref, mask_ref, fgain_ref, sgain_ref, out_ref):
    lower, upper = lower_ref[...], upper_ref[...]
    half = BLOCK // 2
    wide = 3 * BLOCK
    for r in range(BLOCK):
        before = dyn_ref[:, r * wide : r * wide + BLOCK] * lower
        own = dyn_ref[:, r * wide + BLOCK : r * wide + 2 * BLOCK]
        out_ref[r * STEPS : (r + 1) * STEPS, :] = jnp.concatenate([before, own], axis=1)
    for r in range(half):
        s = r + half
        near = dyn_ref[:, r * wide + 2 * BLOCK : (r + 1) * wide] * upper
        far = dyn_ref[:, s * wide + 2 * BLOCK : (s + 1) * wide] * upper
        out_ref[NA + r * STEPS : NA + (r + 1) * STEPS, :] = jnp.concatenate([near, far], axis=1)
    weight = mask_ref[...].astype(f32) * fgain_ref[...]
    drive = weight * obs_ref[...]
    gain = sgain_ref[...]
    out_ref[NA + NB : NA + NB + STEPS, :] = jnp.concatenate([weight, drive], axis=1)
    out_ref[NA + NB + STEPS :, :] = jnp.concatenate([gain, gain], axis=1)


def forward_kernel(pos_ref, m0, m1, m2, m3, fhi_ref, flo_ref, vec_ref, x_ref):
    place = pos_ref[0]
    zeros64 = jnp.zeros((BLOCK, BLOCK), f32)
    vec_w = vec_d = vec_g = None
    for s, m in enumerate((m0, m1, m2, m3)):
        block = lax.rem(place - s + BLOCKS, BLOCKS)
        shift = lax.rem(block + BLOCKS - 1, BLOCKS) * BLOCK
        rows = pl.ds(pl.multiple_of(block * BLOCK, BLOCK), BLOCK)
        for t in range(STEPS):
            left = m[pl.ds(t, BLOCK, stride=STEPS), :]
            pair = m[pl.ds(NA + t, BLOCK // 2, stride=STEPS), :]
            after = jnp.concatenate([pair[:, :BLOCK], pair[:, BLOCK:]], axis=0)
            full = jnp.concatenate([left, after, zeros64], axis=1)
            hi, lo = split(pltpu.roll(full, shift, 1))
            fhi_ref[t, rows, :] = hi
            flo_ref[t, rows, :] = lo
        wd = m[NA + NB : NA + NB + STEPS, :]
        g = m[NA + NB + STEPS :, :]
        zero = jnp.zeros((STEPS, STATE - BLOCK), f32)
        place_at = block * BLOCK
        w_part = pltpu.roll(jnp.concatenate([wd[:, :BLOCK], zero], axis=1), place_at, 1)
        d_part = pltpu.roll(jnp.concatenate([wd[:, BLOCK:], zero], axis=1), place_at, 1)
        g_part = pltpu.roll(jnp.concatenate([g[:, :BLOCK], zero], axis=1), place_at, 1)
        vec_w = w_part if vec_w is None else vec_w + w_part
        vec_d = d_part if vec_d is None else vec_d + d_part
        vec_g = g_part if vec_g is None else vec_g + g_part
    vec_ref[0] = vec_w
    vec_ref[1] = vec_d
    vec_ref[2] = vec_g
    state = jnp.concatenate([identity_matrix(), jnp.zeros((8, STATE), f32)], axis=0)
    for t in range(STEPS):
        state = three(dot_nt, split(state), (fhi_ref[t], flo_ref[t])) * (1.0 - vec_w[t : t + 1])
        state = jnp.concatenate(
            [state[:STATE], state[STATE:] + first_row(vec_d[t : t + 1])], axis=0
        )
    x_ref[...] = state


def composite_kernel(fhi_ref, flo_ref, vec_ref, y_ref, z_ref):
    x = jnp.concatenate([identity_matrix(), jnp.zeros((8, STATE), f32)], axis=0)
    y = identity_matrix()
    z = jnp.zeros((AUG, STATE), f32)
    for t in range(STEPS):
        w, d, g = vec_ref[0, t : t + 1, :], vec_ref[1, t : t + 1, :], vec_ref[2, t : t + 1, :]
        step = (fhi_ref[t], flo_ref[t])
        moved = three(dot_nt, split(x), step)
        back = three(dot_nt, split(y), step)
        drive = first_row(d)
        kept = moved * (1.0 - w)
        taken = -(moved * w)
        x = jnp.concatenate([kept[:STATE], kept[STATE:] + drive], axis=0)
        right = jnp.concatenate([taken[:STATE], taken[STATE:] + drive], axis=0)
        z = z + mul_nt(right, back)
        y = back * g
    y_ref[...] = y
    z_ref[...] = z


def then(first, second):
    both = mul_nn(first, second[:STATE])
    return jnp.concatenate([both[:STATE], both[STATE:] + second[STATE:]], axis=0)


def pair_forward_kernel(pos_ref, own_ref, other_ref, x_ref):
    own, other = own_ref[...], other_ref[...]
    lead = pos_ref[3] == 0
    x_ref[...] = then(jnp.where(lead, own, other), jnp.where(lead, other, own))


def pair_back_kernel(pos_ref, x_own, x_other, yz_own, yz_other, y_ref, z_ref):
    lead = pos_ref[3] == 0
    xl = jnp.where(lead, x_own[...], x_other[...])
    yl = jnp.where(lead, yz_own[:STATE], yz_other[:STATE])
    yr = jnp.where(lead, yz_other[:STATE], yz_own[:STATE])
    zl = jnp.where(lead, yz_own[STATE:], yz_other[STATE:])
    zr = jnp.where(lead, yz_other[STATE:], yz_own[STATE:])
    y_ref[...] = mul_nn(yl, yr)
    inner = then(xl, zr)
    z_ref[...] = zl + mul_nt(inner, yl)


def ordered(scratch, refs, place):
    for s, ref in enumerate(refs):
        scratch[lax.rem(place - s + 4, 4)] = ref[...]


def row_forward_kernel(pos_ref, a0, a1, a2, a3, whole_ref, before_ref, scr):
    x = pos_ref[1]
    ordered(scr, (a0, a1, a2, a3), x)
    run = scr[0]
    before = jnp.concatenate([identity_matrix(), jnp.zeros((8, STATE), f32)], axis=0)
    before = jnp.where(x == 1, run, before)
    for i in range(1, 4):
        run = then(run, scr[i])
        if i < 3:
            before = jnp.where(x == i + 1, run, before)
    whole_ref[...] = run
    before_ref[...] = before


def enter_kernel(
    pos_ref, r0, r1, r2, r3, before_ref, x_own, x_other, z_chip, yz_own, yz_other,
    enter_ref, vchip_ref, mid_ref, scr,
):
    y = pos_ref[2]
    ordered(scr, (r0, r1, r2, r3), y)
    m = jnp.zeros((8, STATE), f32)
    for g in range(3):
        u = scr[g, STATE:, :]
        after = u if g == 0 else mul_nn(m, scr[g, :STATE, :]) + u
        m = jnp.where(y > g, after, m)
    m = mul_nn(m, before_ref[:STATE]) + before_ref[STATE:]
    lead = pos_ref[3] == 0
    x_lead = jnp.where(lead, x_own[...], x_other[...])
    mid = mul_nn(m, x_lead[:STATE]) + x_lead[STATE:]
    enter_ref[...] = jnp.where(lead, m, mid)
    vchip_ref[...] = mul_nn(m, z_chip[:STATE]) + z_chip[STATE:]
    z_last = jnp.where(lead, yz_other[STATE:], yz_own[STATE:])
    mid_ref[...] = mul_nn(mid, z_last[:STATE]) + z_last[STATE:]


def row_back_kernel(pos_ref, y0, y1, y2, y3, whole_ref, after_ref, scr):
    x = pos_ref[1]
    ordered(scr, (y0, y1, y2, y3), x)
    run = scr[3]
    after = jnp.where(x == 2, run, identity_matrix())
    for i in (2, 1, 0):
        run = mul_nn(scr[i], run)
        if i > 0:
            after = jnp.where(x == i - 1, run, after)
    whole_ref[...] = run
    after_ref[...] = after


def row_v_kernel(pos_ref, v0, v1, v2, v3, y0, y1, y2, y3, whole_ref, after_ref, vscr, yscr):
    x = pos_ref[1]
    ordered(vscr, (v0, v1, v2, v3), x)
    ordered(yscr, (y0, y1, y2, y3), x)
    run = vscr[3]
    after = jnp.where(x == 2, run, 0.0)
    for i in (2, 1, 0):
        run = vscr[i] + mul_nt(run, yscr[i])
        if i > 0:
            after = jnp.where(x == i - 1, run, after)
    whole_ref[...] = run
    after_ref[...] = after


def local_kernel(enter_ref, fhi_ref, flo_ref, vec_ref, m_ref, e_ref):
    m = enter_ref[...]
    for t in range(STEPS):
        w, d = vec_ref[0, t : t + 1, :], vec_ref[1, t : t + 1, :]
        p = three(dot_nt, split(m), (fhi_ref[t], flo_ref[t]))
        e = first_row(d) - w * p
        m = p + e
        m_ref[t : t + 1, :] = m[0:1]
        e_ref[t : t + 1, :] = e[0:1]


def smooth_kernel(
    pos_ref, v0, v1, v2, v3, y0, y1, y2, y3, yafter_ref, vafter_ref, yz_other, mid_ref,
    fhi_ref, flo_ref, vec_ref, m_ref, e_ref, filt_ref, smooth_ref, vscr, yscr,
):
    place = pos_ref[0]
    y = pos_ref[2]
    ordered(vscr, (v0, v1, v2, v3), y)
    ordered(yscr, (y0, y1, y2, y3), y)
    sigma = jnp.zeros((8, STATE), f32)
    for g in (3, 2, 1):
        after = vscr[g] if g == 3 else mul_nt(sigma, yscr[g]) + vscr[g]
        sigma = jnp.where(y < g, after, sigma)
    sigma = mul_nt(sigma, yafter_ref[...]) + vafter_ref[...]
    crossed = mul_nt(sigma, yz_other[:STATE]) + mid_ref[...]
    sigma = jnp.where(pos_ref[3] == 0, crossed, sigma)
    rows = [None] * STEPS
    for t in range(STEPS - 1, -1, -1):
        q = vec_ref[2, t : t + 1, :] * sigma
        rows[t] = m_ref[t : t + 1, :] + q[0:1]
        if t > 0:
            sigma = three(
                dot_nn, split(q + first_row(e_ref[t : t + 1, :])), (fhi_ref[t], flo_ref[t])
            )
    smooth = jnp.concatenate(rows, axis=0)
    filt = m_ref[...]
    out_f = filt[:, :BLOCK]
    out_s = smooth[:, :BLOCK]
    for b in range(1, BLOCKS):
        part = slice(b * BLOCK, (b + 1) * BLOCK)
        out_f = jnp.where(place == b, filt[:, part], out_f)
        out_s = jnp.where(place == b, smooth[:, part], out_s)
    filt_ref[...] = out_f
    smooth_ref[...] = out_s


def over_z(a, s):
    return lax.ppermute(a, "state", [(i, (i + s) % 4) for i in range(4)])


def over_core(a):
    return lax.ppermute(a, "tm", [(i, i ^ 1) for i in range(32)])


def chip(x, y, c):
    return (y * 4 + x) * 2 + c


CHIPS = [(x, y, c) for y in range(4) for x in range(4) for c in range(2)]


def over_x(a, s):
    return lax.ppermute(a, "tm", [(chip(x, y, c), chip((x + s) % 4, y, c)) for x, y, c in CHIPS])


def over_y(a, s):
    return lax.ppermute(a, "tm", [(chip(x, y, c), chip(x, (y + s) % 4, c)) for x, y, c in CHIPS])


def gather(move, a):
    return [a] + [move(a, s) for s in (1, 2, 3)]


def shards(dynamics, band, observed, obs_mask, filter_gain, smooth_gain):
    z = lax.axis_index("state")
    tm = lax.axis_index("tm")
    pos = jnp.stack([z, (tm // 2) % 4, tm // 8, tm % 2]).astype(jnp.int32)
    lower = jnp.where(z > 0, band[:, :, 0], 0).astype(f32)
    upper = jnp.where(z < BLOCKS - 1, band[:, :, 1], 0).astype(f32)
    (packed,) = call(
        pack_kernel,
        [arr(PACKED, 128)],
        [dynamics, lower, upper, observed, obs_mask, filter_gain, smooth_gain],
    )
    parts = gather(over_z, packed)
    fhi, flo, vec, x_own = call(
        forward_kernel,
        [arr(STEPS, STATE, STATE, dtype=bf16)] * 2 + [arr(3, STEPS, STATE), arr(AUG, STATE)],
        [pos] + parts,
    )
    x_other = over_core(x_own)
    (x_chip,) = call(pair_forward_kernel, [arr(AUG, STATE)], [pos, x_own, x_other])
    x_chips = gather(over_x, x_chip)
    y_own, z_own = call(
        composite_kernel, [arr(STATE, STATE), arr(AUG, STATE)], [fhi, flo, vec]
    )
    yz_own = jnp.concatenate([y_own, z_own], axis=0)
    yz_other = over_core(yz_own)
    y_chip, z_chip = call(
        pair_back_kernel,
        [arr(STATE, STATE), arr(AUG, STATE)],
        [pos, x_own, x_other, yz_own, yz_other],
    )
    x_row, x_before = call(
        row_forward_kernel,
        [arr(AUG, STATE)] * 2,
        [pos] + x_chips,
        [pltpu.VMEM((4, AUG, STATE), f32)],
    )
    x_rows = gather(over_y, x_row)
    y_chips = gather(over_x, y_chip)
    enter, v_chip, v_mid = call(
        enter_kernel,
        [arr(8, STATE)] * 3,
        [pos] + x_rows + [x_before, x_own, x_other, z_chip, yz_own, yz_other],
        [pltpu.VMEM((4, AUG, STATE), f32)],
    )
    v_chips = gather(over_x, v_chip)
    y_row, y_after = call(
        row_back_kernel,
        [arr(STATE, STATE)] * 2,
        [pos] + y_chips,
        [pltpu.VMEM((4, STATE, STATE), f32)],
    )
    y_rows = gather(over_y, y_row)
    m_all, e_all = call(local_kernel, [arr(STEPS, STATE)] * 2, [enter, fhi, flo, vec])
    v_row, v_after = call(
        row_v_kernel,
        [arr(8, STATE)] * 2,
        [pos] + v_chips + y_chips,
        [pltpu.VMEM((4, 8, STATE), f32), pltpu.VMEM((4, STATE, STATE), f32)],
    )
    v_rows = gather(over_y, v_row)
    filtered, smoothed = call(
        smooth_kernel,
        [arr(STEPS, BLOCK)] * 2,
        [pos] + v_rows + y_rows + [y_after, v_after, yz_other, v_mid, fhi, flo, vec, m_all, e_all],
        [pltpu.VMEM((4, 8, STATE), f32), pltpu.VMEM((4, STATE, STATE), f32)],
    )
    return filtered, smoothed


def solution(mesh):
    in_specs = (
        P("tm", "state"),
        P("tm", "state", None),
        P("tm", "state"),
        P("tm", "state"),
        P("tm", "state"),
        P("tm", "state"),
    )
    out_specs = (P("tm", "state"), P("tm", "state"))
    return jax.shard_map(shards, mesh=mesh, in_specs=in_specs, out_specs=out_specs, check_vma=False)
```

```python
import functools

import jax
import jax.numpy as jnp
from jax import lax
from jax.experimental import pallas as pl
from jax.experimental.pallas import tpu as pltpu
from jax.sharding import PartitionSpec as P

BLOCK = 64
STATE = 256
BLOCKS = 4
STEPS = 16
SIZES = (4, 4, 4, 4)
RELAYS = (1, 1, 3, 3)
CHUNKS = len(SIZES)
STARTS = tuple(sum(SIZES[:q]) for q in range(CHUNKS))
AUG = STATE + 8
MIB = 1 << 20

f32 = jnp.float32
bf16 = jnp.bfloat16


def split(a):
    hi = a.astype(bf16)
    return hi, (a - hi.astype(f32)).astype(bf16)


def dot_nn(a, b):
    return lax.dot_general(a, b, (((1,), (0,)), ((), ())), preferred_element_type=f32)


def dot_nt(a, b):
    return lax.dot_general(a, b, (((1,), (1,)), ((), ())), preferred_element_type=f32)


def three(dot, a, b):
    ahi, alo = a
    bhi, blo = b
    return dot(ahi, bhi) + (dot(alo, bhi) + dot(ahi, blo))


def rows_by(dot, a, b):
    high = a.astype(bf16).astype(f32)
    both = jnp.concatenate([high, a - high], axis=0).astype(bf16)
    wide = dot(both, b[0]) + dot(both, b[1])
    return wide[:8] + wide[8:]


def mul_by(dot, a, b):
    if a.shape[0] == 8:
        return rows_by(dot, a, split(b))
    return three(dot, split(a), split(b))


def mul_nn(a, b):
    return mul_by(dot_nn, a, b)


def mul_nt(a, b):
    return mul_by(dot_nt, a, b)


def first_row(row):
    spread = jnp.broadcast_to(row, (8, row.shape[1]))
    return jnp.where(lax.broadcasted_iota(jnp.int32, spread.shape, 0) == 0, spread, 0.0)


def identity_matrix():
    rows = lax.broadcasted_iota(jnp.int32, (STATE, STATE), 0)
    cols = lax.broadcasted_iota(jnp.int32, (STATE, STATE), 1)
    return jnp.where(rows == cols, 1.0, 0.0).astype(f32)


def call(kernel, us, outs, args, scratch=(), raw=False, limit=40):
    vmem = pl.BlockSpec(memory_space=pltpu.VMEM)
    moved = sum(a.size * a.dtype.itemsize for a in args) + sum(
        o.size * o.dtype.itemsize for o in outs
    )
    return pl.pallas_call(
        kernel,
        out_shape=outs,
        in_specs=[pl.BlockSpec(memory_space=pltpu.HBM) if raw else vmem] * len(args),
        out_specs=[vmem] * len(outs),
        scratch_shapes=list(scratch),
        compiler_params=pltpu.CompilerParams(vmem_limit_bytes=limit * MIB),
        cost_estimate=pl.CostEstimate(flops=int(us * 1e9), bytes_accessed=moved, transcendentals=0),
    )(*args)


def arr(*shape, dtype=f32):
    return jax.ShapeDtypeStruct(shape, dtype)


def core_of():
    return lax.rem(lax.axis_index("tm"), 2)


def x_of():
    return lax.rem(lax.axis_index("tm") // 2, 4)


def y_of():
    return lax.axis_index("tm") // 8


PER_STEP = BLOCK + BLOCK // 2 + 2
PART_Y = AUG
ROWS = 2 * AUG
ENDS = tuple((q, i) for q in range(CHUNKS) for i in range(SIZES[q]))


def pack_kernel(dyn_hbm, band_hbm, obs_hbm, mask_hbm, fgain_hbm, sgain_hbm, *refs):
    outs = refs[:CHUNKS]
    dyn_ref, band_ref, obs_ref, mask_ref, fgain_ref, sgain_ref, sems = refs[CHUNKS:]
    copies = [
        pltpu.make_async_copy(src, dst, sems.at[i])
        for i, (src, dst) in enumerate(
            (
                (dyn_hbm, dyn_ref),
                (band_hbm, band_ref),
                (obs_hbm, obs_ref),
                (mask_hbm, mask_ref),
                (fgain_hbm, fgain_ref),
                (sgain_hbm, sgain_ref),
            )
        )
    ]
    for copy in copies:
        copy.start()
    for copy in copies:
        copy.wait()
    place = lax.axis_index("state")
    row = lax.broadcasted_iota(jnp.int32, (2, STEPS), 0)
    outside = jnp.where(place == 0, 0, jnp.where(place == BLOCKS - 1, 1, 2))
    band = jnp.where(row == outside, 0, band_ref[...]).astype(f32)
    band = jnp.transpose(jnp.concatenate([band, jnp.zeros((6, STEPS), f32)], axis=0))
    lower, upper = band[:, 0:1], band[:, 1:2]
    half = BLOCK // 2
    wide = 3 * BLOCK

    def put(at, value):
        for t0, size, out in zip(STARTS, SIZES, outs):
            out[at * size : (at + 1) * size, :] = value[t0 : t0 + size]

    for r in range(BLOCK):
        before = dyn_ref[:, r * wide : r * wide + BLOCK] * lower
        own = dyn_ref[:, r * wide + BLOCK : r * wide + 2 * BLOCK]
        put(r, jnp.concatenate([before, own], axis=1))
    for r in range(half):
        s = r + half
        near = dyn_ref[:, r * wide + 2 * BLOCK : (r + 1) * wide] * upper
        far = dyn_ref[:, s * wide + 2 * BLOCK : (s + 1) * wide] * upper
        put(BLOCK + r, jnp.concatenate([near, far], axis=1))
    weight = mask_ref[...].astype(f32) * fgain_ref[...]
    gain = sgain_ref[...]
    put(BLOCK + half, jnp.concatenate([weight, obs_ref[...]], axis=1))
    put(BLOCK + half + 1, jnp.concatenate([gain, gain], axis=1))


def chunk_kernel(first, size, *refs):
    parts = refs[:BLOCKS]
    state_ref, fhi_ref, flo_ref, thi_ref, tlo_ref, vec_ref, out_ref = (
        (None,) if first else ()
    ) + refs[BLOCKS:]
    place = lax.axis_index("state")
    zeros64 = jnp.zeros((BLOCK, BLOCK), f32)
    zero = jnp.zeros((size, STATE - BLOCK), f32)
    vecs = [None] * 3
    pairs_at = BLOCK * size
    vecs_at = pairs_at + BLOCK // 2 * size
    for s, m in enumerate(parts):
        block = lax.rem(place - s + BLOCKS, BLOCKS)
        shift = lax.rem(block + BLOCKS - 1, BLOCKS) * BLOCK
        rows = pl.ds(pl.multiple_of(block * BLOCK, BLOCK), BLOCK)
        for t in range(size):
            left = m[pl.ds(t, BLOCK, stride=size), :]
            pair = m[pl.ds(pairs_at + t, BLOCK // 2, stride=size), :]
            after = jnp.concatenate([pair[:, :BLOCK], pair[:, BLOCK:]], axis=0)
            full = jnp.concatenate([left, after, zeros64], axis=1)
            hi, lo = split(pltpu.roll(full, shift, 1))
            fhi_ref[t, rows, :] = hi
            flo_ref[t, rows, :] = lo
        wo = m[vecs_at : vecs_at + size, :]
        g = m[vecs_at + size : vecs_at + 2 * size, :]
        for i, piece in enumerate((wo[:, :BLOCK], wo[:, BLOCK:], g[:, :BLOCK])):
            piece = pltpu.roll(jnp.concatenate([piece, zero], axis=1), block * BLOCK, 1)
            vecs[i] = piece if vecs[i] is None else vecs[i] + piece
    for i in range(3):
        vec_ref[i] = vecs[i]
    if first:
        x = jnp.concatenate([identity_matrix(), jnp.zeros((8, STATE), f32)], axis=0)
        y = identity_matrix()
    else:
        x = state_ref[:AUG]
        y = state_ref[PART_Y : PART_Y + STATE]
    for t in range(size):
        w, o, g = (vecs[i][t : t + 1, :] for i in range(3))
        step = (fhi_ref[t], flo_ref[t])
        moved = three(dot_nt, split(x), step)
        thi_ref[t], tlo_ref[t] = split(moved[:STATE])
        vec_ref[3, t : t + 1, :] = moved[STATE : STATE + 1]
        kept = moved * (1.0 - w)
        x = jnp.concatenate([kept[:STATE], kept[STATE:] + first_row(w * o)], axis=0)
        y = three(dot_nt, split(y), step) * g
    out_ref[:AUG] = x
    out_ref[PART_Y : PART_Y + STATE] = y
    out_ref[PART_Y + STATE :] = jnp.zeros((8, STATE), f32)


def then(first, second):
    both = mul_nn(first, second[:STATE])
    return jnp.concatenate([both[:STATE], both[STATE:] + second[STATE:]], axis=0)


def pair_kernel(own_ref, other_ref, out_ref):
    core = core_of()
    part = pl.ds(pl.multiple_of(core * AUG, 8), AUG)
    own, other = own_ref[part, :], other_ref[part, :]
    lead = core == 0
    out_ref[...] = then(jnp.where(lead, own, other), jnp.where(lead, other, own))


def pair_z_kernel(own_ref, other_ref, z_own, z_other, z_ref):
    lead = core_of() == 0
    xl = jnp.where(lead, own_ref[:AUG], other_ref[:AUG])
    yl = jnp.where(lead, own_ref[PART_Y : PART_Y + STATE], other_ref[PART_Y : PART_Y + STATE])
    zl = jnp.where(lead, z_own[...], z_other[...])
    zr = jnp.where(lead, z_other[...], z_own[...])
    z_ref[...] = zl + mul_nt(then(xl, zr), yl)


def suffix_kernel(*refs):
    his, los, vecs = (refs[i * CHUNKS : (i + 1) * CHUNKS] for i in range(3))
    shi_ref, slo_ref = refs[-2:]
    run = identity_matrix()
    for t in range(STEPS - 1, 0, -1):
        q, i = ENDS[t]
        run = three(dot_nn, split(run * vecs[q][2, i : i + 1, :]), (his[q][i], los[q][i]))
        shi_ref[t], slo_ref[t] = split(run)


def suffix_z_kernel(*refs):
    his, los, this, tlos, vecs = (refs[i * CHUNKS : (i + 1) * CHUNKS] for i in range(5))
    zhi_ref, zlo_ref, v_ref, z_ref = refs[5 * CHUNKS :]
    z = jnp.zeros((STATE, STATE), f32)
    v = jnp.zeros((8, STATE), f32)
    v_ref[...] = jnp.zeros((STEPS, STATE), f32)
    for t in range(STEPS - 1, -1, -1):
        q, i = ENDS[t]
        w, o, g, p = (vecs[q][k, i : i + 1, :] for k in range(4))
        step = (his[q][i], los[q][i])
        moved = this[q][i].astype(f32) + tlos[q][i].astype(f32)
        z = three(dot_nn, split(z * g - moved * w), step)
        v = rows_by(dot_nn, v * g + first_row(w * (o - p)), step)
        if t > 0:
            zhi_ref[t], zlo_ref[t] = split(z)
            v_ref[t : t + 1, :] = v[0:1]
    z_ref[:STATE] = z
    z_ref[STATE:] = v


def duo_kernel(own, partner, _, out_ref):
    even = lax.rem(x_of(), 2) == 0
    mine, theirs = own[...], partner[...]
    out_ref[...] = then(jnp.where(even, mine, theirs), jnp.where(even, theirs, mine))


def row_kernel(partner, duo, other_duo, *refs):
    whole_ref, side_ref, tail_ref = refs[-3:]
    x = x_of()
    lead = core_of() == 0
    low = x < 2
    mine, theirs, beside = duo[...], other_duo[...], partner[...]
    whole = then(jnp.where(low, mine, theirs), jnp.where(low, theirs, mine))
    whole_ref[...] = whole
    tail_ref[...] = whole[STATE:]
    outer = then(jnp.where(lead, theirs, beside), jnp.where(lead, beside, theirs))
    nothing = jnp.concatenate([identity_matrix(), jnp.zeros((8, STATE), f32)], axis=0)
    depth = jnp.where(lead, x, 3 - x)
    side = jnp.where(depth == 0, nothing, jnp.where(depth == 1, beside, theirs))
    side_ref[...] = jnp.where(depth == 3, outer, side)


def enter_kernel(near, far, tail, side_ref, own_ref, z_chip, means_ref, v_ref):
    y = y_of()
    through = mul_nn(tail[...], far[:STATE]) + far[STATE:]
    inner = jnp.where(y == 3, through, jnp.where(y == 2, far[STATE:], 0.0))
    m = mul_nn(inner, near[:STATE]) + near[STATE:]
    m = mul_nn(m, side_ref[:STATE]) + side_ref[STATE:]
    v = mul_nn(m, z_chip[:STATE]) + z_chip[STATE:]
    v_ref[...] = v
    means_ref[:8] = v
    means_ref[8:16] = m
    means_ref[16:] = mul_nn(m, own_ref[:STATE]) + own_ref[STATE:AUG]


def local_kernel(means_ref, sent_ref, z_other, zhi_ref, zlo_ref, v_ref, *refs):
    this, tlos, vecs = (refs[i * CHUNKS : (i + 1) * CHUNKS] for i in range(3))
    m_ref, h_ref, mid_ref = refs[3 * CHUNKS :]
    mid_ref[...] = mul_nn(means_ref[16:], z_other[:STATE]) + z_other[STATE:]
    enter = jnp.where(core_of() == 0, means_ref[8:16], sent_ref[16:])
    for q in range(CHUNKS):
        rows = [rows_by(dot_nn, enter, (this[q][i], tlos[q][i]))[0:1] for i in range(SIZES[q])]
        p = jnp.concatenate(rows, axis=0) + vecs[q][3]
        e = vecs[q][0] * (vecs[q][1] - p)
        m_ref[STARTS[q] : STARTS[q] + SIZES[q], :] = p + e
    for t in range(STEPS - 1):
        row = rows_by(dot_nn, enter, (zhi_ref[t + 1], zlo_ref[t + 1]))[0:1]
        h_ref[t : t + 1, :] = row + v_ref[t + 1 : t + 2, :]
    h_ref[STEPS - 1 :, :] = jnp.zeros((1, STATE), f32)


def duo_v_kernel(sent, partner_v, own_y, partner_y, _, out_ref):
    even = lax.rem(x_of(), 2) == 0
    mine, theirs = sent[:8], partner_v[...]
    y = jnp.where(even, own_y[:STATE], partner_y[:STATE])
    out_ref[...] = jnp.where(even, mine, theirs) + mul_nt(jnp.where(even, theirs, mine), y)


def row_v_kernel(duo_v, other_v, partner_v, duo_y, other_y, partner_y, whole_ref, after_ref):
    x = x_of()
    low = x < 2
    mine, theirs, beside = duo_v[...], other_v[...], partner_v[...]
    y = jnp.where(low, duo_y[:STATE], other_y[:STATE])
    whole_ref[...] = jnp.where(low, mine, theirs) + mul_nt(jnp.where(low, theirs, mine), y)
    outer = beside + mul_nt(theirs, partner_y[:STATE])
    after = jnp.where(x == 3, 0.0, jnp.where(x == 2, beside, theirs))
    after_ref[...] = jnp.where(x == 0, outer, after)


def leave_kernel(v1, v2, v3, near, far, side_ref, after_ref, *refs):
    out_ref = refs[-1]
    inner = v2[...] + mul_nt(v3[...], far[:STATE])
    sigma = v1[...] + mul_nt(inner, near[:STATE])
    out_ref[...] = mul_nt(sigma, side_ref[:STATE]) + after_ref[...]


def smooth_kernel(sigma_ref, sent_ref, other_ref, mid_ref, shi_ref, slo_ref, *refs):
    vecs = refs[:CHUNKS]
    m_ref, h_ref, filt_ref, smooth_ref = refs[CHUNKS:]
    place = lax.axis_index("state")
    crossed = mul_nt(sent_ref[...], other_ref[PART_Y : PART_Y + STATE]) + mid_ref[...]
    sigma = jnp.where(core_of() == 0, crossed, sigma_ref[...])
    rows = []
    for t in range(STEPS):
        if t == STEPS - 1:
            rows.append(sigma[0:1])
        else:
            rows.append(rows_by(dot_nn, sigma, (shi_ref[t + 1], slo_ref[t + 1]))[0:1])
    gain = jnp.concatenate([v[2] for v in vecs], axis=0)
    filt = m_ref[...]
    smooth = filt + gain * (h_ref[...] + jnp.concatenate(rows, axis=0))
    out_f = filt[:, :BLOCK]
    out_s = smooth[:, :BLOCK]
    for b in range(1, BLOCKS):
        part = slice(b * BLOCK, (b + 1) * BLOCK)
        out_f = jnp.where(place == b, filt[:, part], out_f)
        out_s = jnp.where(place == b, smooth[:, part], out_s)
    filt_ref[...] = out_f
    smooth_ref[...] = out_s


def over_z(a, s):
    return lax.ppermute(a, "state", [(i, (i + s) % 4) for i in range(4)])


def chip(x, y, c):
    return (y * 4 + x) * 2 + c


def over_core(a):
    return lax.ppermute(a, "tm", [(i, i ^ 1) for i in range(32)])


def over_x(a, to, pairs=((0, 0), (1, 1))):
    route = [
        (chip(x, y, c), chip(to(x), y, d)) for y in range(4) for x in range(4) for c, d in pairs
    ]
    return lax.ppermute(a, "tm", route)


def beside(x):
    return x ^ 1


def opposite(x):
    return 3 - x


def over_y(a, up=(), down=()):
    route = [(chip(x, a, 0), chip(x, b, 0)) for a, b in up for x in range(4)]
    route += [(chip(x, a, 1), chip(x, b, 1)) for a, b in down for x in range(4)]
    return lax.ppermute(a, "tm", route)


def gather_z(chunks):
    ahead = [over_z(a, 1) for a in chunks]
    behind = [over_z(a, 3) for a in chunks]
    return [
        [a, ahead[q], over_z(ahead[q] if RELAYS[q] == 1 else behind[q], RELAYS[q]), behind[q]]
        for q, a in enumerate(chunks)
    ]


def shards(dynamics, band, observed, obs_mask, filter_gain, smooth_gain):
    packed = call(
        pack_kernel,
        0,
        [arr(PER_STEP * size, 128) for size in SIZES],
        [dynamics, band.transpose(1, 2, 0).reshape(2, STEPS), observed, obs_mask, filter_gain, smooth_gain],
        [
            pltpu.VMEM((STEPS, 3 * BLOCK * BLOCK), f32),
            pltpu.VMEM((2, STEPS), jnp.int32),
            pltpu.VMEM((STEPS, BLOCK), f32),
            pltpu.VMEM((STEPS, BLOCK), jnp.int32),
            pltpu.VMEM((STEPS, BLOCK), f32),
            pltpu.VMEM((STEPS, BLOCK), f32),
            pltpu.SemaphoreType.DMA((6,)),
        ],
        raw=True,
        limit=60,
    )
    his, los, this, tlos, vecs, state = [], [], [], [], [], []
    for q, parts in enumerate(gather_z(packed)):
        size = SIZES[q]
        kept = call(
            functools.partial(chunk_kernel, q == 0, size),
            0.4 * size,
            [arr(size, STATE, STATE, dtype=bf16)] * 4 + [arr(4, size, STATE), arr(ROWS, STATE)],
            parts + state,
        )
        for store, value in zip((his, los, this, tlos, vecs), kept):
            store.append(value)
        own = kept[-1]
        state = [own]
    other = over_core(own)
    (side_own,) = call(pair_kernel, 0, [arr(AUG, STATE)], [own, other])
    partner = over_x(side_own, beside)
    zhi, zlo, v_all, z_own = call(
        suffix_z_kernel,
        0,
        [arr(STEPS, STATE, STATE, dtype=bf16)] * 2 + [arr(STEPS, STATE), arr(AUG, STATE)],
        his + los + this + tlos + vecs,
    )
    (duo,) = call(duo_kernel, 0, [arr(AUG, STATE)], [side_own, partner, z_own])
    other_duo = over_x(duo, opposite)
    z_other = over_core(z_own)
    shi, slo = call(
        suffix_kernel, 0, [arr(STEPS, STATE, STATE, dtype=bf16)] * 2, his + los + vecs
    )
    whole, side, tail = call(
        row_kernel,
        0,
        [arr(AUG, STATE)] * 2 + [arr(8, STATE)],
        [partner, duo, other_duo, z_other, shi],
    )
    tail = over_y(tail, ((0, 3),))
    near = over_y(whole, ((0, 1), (1, 2), (2, 3)), ((2, 1), (1, 0)))
    far = over_y(whole, ((0, 2), (1, 3)), ((2, 0),))
    (z_chip,) = call(pair_z_kernel, 0, [arr(AUG, STATE)], [own, other, z_own, z_other])
    means, v_chip = call(
        enter_kernel,
        0,
        [arr(24, STATE), arr(8, STATE)],
        [near, far, tail, side, own, z_chip],
    )
    partner_v = over_x(v_chip, beside, ((0, 1),))
    sent = over_core(means)
    m_all, h_all, mid = call(
        local_kernel,
        0,
        [arr(STEPS, STATE)] * 2 + [arr(8, STATE)],
        [means, sent, z_other, zhi, zlo, v_all] + this + tlos + vecs,
    )
    (duo_v,) = call(
        duo_v_kernel, 0, [arr(8, STATE)], [sent, partner_v, side_own, partner, h_all]
    )
    other_v = over_x(duo_v, opposite, ((1, 1),))
    v_row, v_after = call(
        row_v_kernel,
        0,
        [arr(8, STATE)] * 2,
        [duo_v, other_v, partner_v, duo, other_duo, partner],
    )
    v_rows = [
        over_y(v_row, (), ((3, 2), (2, 1), (1, 0))),
        over_y(v_row, (), ((3, 1), (2, 0))),
        over_y(v_row, (), ((3, 0),)),
    ]
    (sigma,) = call(leave_kernel, 0, [arr(8, STATE)], v_rows + [near, far, side, v_after])
    crossed = over_core(sigma)
    filtered, smoothed = call(
        smooth_kernel,
        0,
        [arr(STEPS, BLOCK)] * 2,
        [sigma, crossed, other, mid, shi, slo] + vecs + [m_all, h_all],
    )
    return filtered, smoothed


def solution(mesh):
    in_specs = (
        P("tm", "state"),
        P("tm", "state", None),
        P("tm", "state"),
        P("tm", "state"),
        P("tm", "state"),
        P("tm", "state"),
    )
    out_specs = (P("tm", "state"), P("tm", "state"))
    return jax.shard_map(shards, mesh=mesh, in_specs=in_specs, out_specs=out_specs, check_vma=False)
```

```python
import functools

import jax
import jax.numpy as jnp
from jax import lax
from jax.experimental import pallas as pl
from jax.experimental.pallas import tpu as pltpu
from jax.sharding import PartitionSpec as P

BLOCK = 64
STATE = 256
BLOCKS = 4
STEPS = 16
SIZES = (4, 4, 4, 4)
RELAYS = (1, 1, 3, 3)
CHUNKS = len(SIZES)
STARTS = tuple(sum(SIZES[:q]) for q in range(CHUNKS))
AUG = STATE + 8
MIB = 1 << 20

f32 = jnp.float32
bf16 = jnp.bfloat16


def split(a):
    hi = a.astype(bf16)
    return hi, (a - hi.astype(f32)).astype(bf16)


def dot_nn(a, b):
    return lax.dot_general(a, b, (((1,), (0,)), ((), ())), preferred_element_type=f32)


def dot_nt(a, b):
    return lax.dot_general(a, b, (((1,), (1,)), ((), ())), preferred_element_type=f32)


def three(dot, a, b):
    ahi, alo = a
    bhi, blo = b
    return dot(ahi, bhi) + (dot(alo, bhi) + dot(ahi, blo))


def rows_by(dot, a, b):
    high = a.astype(bf16).astype(f32)
    both = jnp.concatenate([high, a - high], axis=0).astype(bf16)
    wide = dot(both, b[0]) + dot(both, b[1])
    return wide[:8] + wide[8:]


def mul_by(dot, a, b):
    if a.shape[0] == 8:
        return rows_by(dot, a, split(b))
    return three(dot, split(a), split(b))


def mul_nn(a, b):
    return mul_by(dot_nn, a, b)


def mul_nt(a, b):
    return mul_by(dot_nt, a, b)


def first_row(row):
    spread = jnp.broadcast_to(row, (8, row.shape[1]))
    return jnp.where(lax.broadcasted_iota(jnp.int32, spread.shape, 0) == 0, spread, 0.0)


def identity_matrix():
    rows = lax.broadcasted_iota(jnp.int32, (STATE, STATE), 0)
    cols = lax.broadcasted_iota(jnp.int32, (STATE, STATE), 1)
    return jnp.where(rows == cols, 1.0, 0.0).astype(f32)


def call(kernel, us, outs, args, scratch=(), raw=False, limit=40):
    vmem = pl.BlockSpec(memory_space=pltpu.VMEM)
    moved = sum(a.size * a.dtype.itemsize for a in args) + sum(
        o.size * o.dtype.itemsize for o in outs
    )
    return pl.pallas_call(
        kernel,
        out_shape=outs,
        in_specs=[pl.BlockSpec(memory_space=pltpu.HBM) if raw else vmem] * len(args),
        out_specs=[vmem] * len(outs),
        scratch_shapes=list(scratch),
        compiler_params=pltpu.CompilerParams(vmem_limit_bytes=limit * MIB),
        cost_estimate=pl.CostEstimate(flops=int(us * 1e9), bytes_accessed=moved, transcendentals=0),
    )(*args)


def arr(*shape, dtype=f32):
    return jax.ShapeDtypeStruct(shape, dtype)


def core_of():
    return lax.rem(lax.axis_index("tm"), 2)


def x_of():
    return lax.rem(lax.axis_index("tm") // 2, 4)


def y_of():
    return lax.axis_index("tm") // 8


PER_STEP = BLOCK + BLOCK // 2 + 2
PART_Y = AUG
ROWS = 2 * AUG
ENDS = tuple((q, i) for q in range(CHUNKS) for i in range(SIZES[q]))


def pack_kernel(dyn_hbm, band_hbm, obs_hbm, mask_hbm, fgain_hbm, sgain_hbm, *refs):
    outs = refs[:CHUNKS]
    dyn_ref, band_ref, obs_ref, mask_ref, fgain_ref, sgain_ref, sems = refs[CHUNKS:]
    copies = [
        pltpu.make_async_copy(src, dst, sems.at[i])
        for i, (src, dst) in enumerate(
            (
                (dyn_hbm, dyn_ref),
                (band_hbm, band_ref),
                (obs_hbm, obs_ref),
                (mask_hbm, mask_ref),
                (fgain_hbm, fgain_ref),
                (sgain_hbm, sgain_ref),
            )
        )
    ]
    for copy in copies:
        copy.start()
    for copy in copies:
        copy.wait()
    place = lax.axis_index("state")
    row = lax.broadcasted_iota(jnp.int32, (2, STEPS), 0)
    outside = jnp.where(place == 0, 0, jnp.where(place == BLOCKS - 1, 1, 2))
    band = jnp.where(row == outside, 0, band_ref[...]).astype(f32)
    band = jnp.transpose(jnp.concatenate([band, jnp.zeros((6, STEPS), f32)], axis=0))
    lower, upper = band[:, 0:1], band[:, 1:2]
    half = BLOCK // 2
    wide = 3 * BLOCK

    def put(at, value):
        for t0, size, out in zip(STARTS, SIZES, outs):
            out[at * size : (at + 1) * size, :] = value[t0 : t0 + size]

    for r in range(BLOCK):
        before = dyn_ref[:, r * wide : r * wide + BLOCK] * lower
        own = dyn_ref[:, r * wide + BLOCK : r * wide + 2 * BLOCK]
        put(r, jnp.concatenate([before, own], axis=1))
    for r in range(half):
        s = r + half
        near = dyn_ref[:, r * wide + 2 * BLOCK : (r + 1) * wide] * upper
        far = dyn_ref[:, s * wide + 2 * BLOCK : (s + 1) * wide] * upper
        put(BLOCK + r, jnp.concatenate([near, far], axis=1))
    weight = mask_ref[...].astype(f32) * fgain_ref[...]
    gain = sgain_ref[...]
    put(BLOCK + half, jnp.concatenate([weight, obs_ref[...]], axis=1))
    put(BLOCK + half + 1, jnp.concatenate([gain, gain], axis=1))


def chunk_kernel(first, size, *refs):
    parts = refs[:BLOCKS]
    state_ref, fhi_ref, flo_ref, thi_ref, tlo_ref, vec_ref, out_ref = (
        (None,) if first else ()
    ) + refs[BLOCKS:]
    place = lax.axis_index("state")
    zeros64 = jnp.zeros((BLOCK, BLOCK), f32)
    zero = jnp.zeros((size, STATE - BLOCK), f32)
    vecs = [None] * 3
    pairs_at = BLOCK * size
    vecs_at = pairs_at + BLOCK // 2 * size
    for s, m in enumerate(parts):
        block = lax.rem(place - s + BLOCKS, BLOCKS)
        shift = lax.rem(block + BLOCKS - 1, BLOCKS) * BLOCK
        rows = pl.ds(pl.multiple_of(block * BLOCK, BLOCK), BLOCK)
        for t in range(size):
            left = m[pl.ds(t, BLOCK, stride=size), :]
            pair = m[pl.ds(pairs_at + t, BLOCK // 2, stride=size), :]
            after = jnp.concatenate([pair[:, :BLOCK], pair[:, BLOCK:]], axis=0)
            full = jnp.concatenate([left, after, zeros64], axis=1)
            hi, lo = split(pltpu.roll(full, shift, 1))
            fhi_ref[t, rows, :] = hi
            flo_ref[t, rows, :] = lo
        wo = m[vecs_at : vecs_at + size, :]
        g = m[vecs_at + size : vecs_at + 2 * size, :]
        for i, piece in enumerate((wo[:, :BLOCK], wo[:, BLOCK:], g[:, :BLOCK])):
            piece = pltpu.roll(jnp.concatenate([piece, zero], axis=1), block * BLOCK, 1)
            vecs[i] = piece if vecs[i] is None else vecs[i] + piece
    for i in range(3):
        vec_ref[i] = vecs[i]
    if first:
        x = jnp.concatenate([identity_matrix(), jnp.zeros((8, STATE), f32)], axis=0)
        y = identity_matrix()
    else:
        x = state_ref[:AUG]
        y = state_ref[PART_Y : PART_Y + STATE]
    for t in range(size):
        w, o, g = (vecs[i][t : t + 1, :] for i in range(3))
        step = (fhi_ref[t], flo_ref[t])
        moved = three(dot_nt, split(x), step)
        thi_ref[t], tlo_ref[t] = split(moved[:STATE])
        vec_ref[3, t : t + 1, :] = moved[STATE : STATE + 1]
        kept = moved * (1.0 - w)
        x = jnp.concatenate([kept[:STATE], kept[STATE:] + first_row(w * o)], axis=0)
        y = three(dot_nt, split(y), step) * g
    out_ref[:AUG] = x
    out_ref[PART_Y : PART_Y + STATE] = y
    out_ref[PART_Y + STATE :] = jnp.zeros((8, STATE), f32)


def then(first, second):
    both = mul_nn(first, second[:STATE])
    return jnp.concatenate([both[:STATE], both[STATE:] + second[STATE:]], axis=0)


def pair_kernel(own_ref, other_ref, out_ref):
    core = core_of()
    part = pl.ds(pl.multiple_of(core * AUG, 8), AUG)
    own, other = own_ref[part, :], other_ref[part, :]
    lead = core == 0
    out_ref[...] = then(jnp.where(lead, own, other), jnp.where(lead, other, own))


def pair_z_kernel(own_ref, other_ref, z_own, z_other, z_ref):
    lead = core_of() == 0
    xl = jnp.where(lead, own_ref[:AUG], other_ref[:AUG])
    yl = jnp.where(lead, own_ref[PART_Y : PART_Y + STATE], other_ref[PART_Y : PART_Y + STATE])
    zl = jnp.where(lead, z_own[...], z_other[...])
    zr = jnp.where(lead, z_other[...], z_own[...])
    z_ref[...] = zl + mul_nt(then(xl, zr), yl)


def own_columns(a):
    place = lax.axis_index("state")
    own = a[:, :BLOCK]
    for b in range(1, BLOCKS):
        own = jnp.where(place == b, a[:, b * BLOCK : (b + 1) * BLOCK], own)
    return own


def own_pair(first, second):
    place = lax.axis_index("state")
    two = 2 * BLOCK
    odd = lax.rem(place, 2) == 1
    first, second = (
        jnp.where(place < 2, a[:, :two], a[:, two:]) for a in (first, second)
    )
    low = jnp.where(odd, pltpu.roll(first, BLOCK, 1), first)
    high = jnp.where(odd, second, pltpu.roll(second, BLOCK, 1))
    lane = lax.broadcasted_iota(jnp.int32, low.shape, 1)
    return jnp.where(lane < BLOCK, low, high)


def put_pair(hi_ref, lo_ref, slot, first, second):
    at = slot % 4 * BLOCK
    part = slice(at, at + 2 * BLOCK)
    hi_ref[slot // 4, :, part], lo_ref[slot // 4, :, part] = split(own_pair(first, second))


def by_steps(row, hi_ref, lo_ref):
    rows = []
    for k in range(STEPS // 4):
        wide = rows_by(dot_nn, row, (hi_ref[k], lo_ref[k]))[0:1]
        rows += [wide[:, i * BLOCK : (i + 1) * BLOCK] for i in range(4)]
    return jnp.concatenate(rows, axis=0)


def suffix_kernel(*refs):
    his, los, vecs = (refs[i * CHUNKS : (i + 1) * CHUNKS] for i in range(3))
    shi_ref, slo_ref = refs[-2:]
    run = held = identity_matrix()
    for t in range(STEPS - 1, 0, -1):
        q, i = ENDS[t]
        run = three(dot_nn, split(run * vecs[q][2, i : i + 1, :]), (his[q][i], los[q][i]))
        if t % 2 == 0:
            held = run
        else:
            put_pair(shi_ref, slo_ref, t - 1, run, held)


def suffix_z_kernel(*refs):
    his, los, this, tlos, vecs = (refs[i * CHUNKS : (i + 1) * CHUNKS] for i in range(5))
    zhi_ref, zlo_ref, thi_ref, tlo_ref, v_ref, z_ref = refs[5 * CHUNKS :]
    z = held = jnp.zeros((STATE, STATE), f32)
    v = jnp.zeros((8, STATE), f32)
    v_ref[...] = jnp.zeros((STEPS, STATE), f32)
    for t in range(STEPS - 1, -1, -1):
        q, i = ENDS[t]
        w, o, g, p = (vecs[q][k, i : i + 1, :] for k in range(4))
        step = (his[q][i], los[q][i])
        moved = this[q][i].astype(f32) + tlos[q][i].astype(f32)
        if t % 2 == 0:
            put_pair(thi_ref, tlo_ref, t, moved, after)
        after = moved
        z = three(dot_nn, split(z * g - moved * w), step)
        v = rows_by(dot_nn, v * g + first_row(w * (o - p)), step)
        if t > 0:
            v_ref[t - 1 : t, :] = v[0:1]
            if t % 2 == 0:
                held = z
            else:
                put_pair(zhi_ref, zlo_ref, t - 1, z, held)
    z_ref[:STATE] = z
    z_ref[STATE:] = v


def duo_kernel(own, partner, _, out_ref):
    even = lax.rem(x_of(), 2) == 0
    mine, theirs = own[...], partner[...]
    out_ref[...] = then(jnp.where(even, mine, theirs), jnp.where(even, theirs, mine))


def row_kernel(partner, duo, other_duo, *refs):
    whole_ref, side_ref, tail_ref = refs[-3:]
    x = x_of()
    lead = core_of() == 0
    low = x < 2
    mine, theirs, beside = duo[...], other_duo[...], partner[...]
    whole = then(jnp.where(low, mine, theirs), jnp.where(low, theirs, mine))
    whole_ref[...] = whole
    tail_ref[...] = whole[STATE:]
    outer = then(jnp.where(lead, theirs, beside), jnp.where(lead, beside, theirs))
    nothing = jnp.concatenate([identity_matrix(), jnp.zeros((8, STATE), f32)], axis=0)
    depth = jnp.where(lead, x, 3 - x)
    side = jnp.where(depth == 0, nothing, jnp.where(depth == 1, beside, theirs))
    side_ref[...] = jnp.where(depth == 3, outer, side)


def enter_kernel(near, far, tail, side_ref, own_ref, z_chip, means_ref, v_ref):
    y = y_of()
    through = mul_nn(tail[...], far[:STATE]) + far[STATE:]
    inner = jnp.where(y == 3, through, jnp.where(y == 2, far[STATE:], 0.0))
    m = mul_nn(inner, near[:STATE]) + near[STATE:]
    m = mul_nn(m, side_ref[:STATE]) + side_ref[STATE:]
    v = mul_nn(m, z_chip[:STATE]) + z_chip[STATE:]
    v_ref[:8] = v
    v_ref[8:] = jnp.zeros((40, STATE), f32)
    means_ref[:8] = v
    means_ref[8:16] = m
    means_ref[16:] = mul_nn(m, own_ref[:STATE]) + own_ref[STATE:AUG]


def local_kernel(
    means_ref, sent_ref, z_other, zhi_ref, zlo_ref, thi_ref, tlo_ref, v_ref, *refs
):
    vecs = refs[:CHUNKS]
    m_ref, h_ref, mid_ref = refs[CHUNKS:]
    mid_ref[...] = mul_nn(means_ref[16:], z_other[:STATE]) + z_other[STATE:]
    enter = jnp.where(core_of() == 0, means_ref[8:16], sent_ref[16:])
    w, o, p = (
        own_columns(jnp.concatenate([v[k] for v in vecs], axis=0)) for k in (0, 1, 3)
    )
    p = by_steps(enter, thi_ref, tlo_ref) + p
    m_ref[...] = p + w * (o - p)
    h_ref[...] = by_steps(enter, zhi_ref, zlo_ref) + own_columns(v_ref[...])


def duo_v_kernel(sent, partner_v, own_y, partner_y, _, out_ref):
    even = lax.rem(x_of(), 2) == 0
    mine, theirs = sent[:8], partner_v[:8]
    y = jnp.where(even, own_y[:STATE], partner_y[:STATE])
    out_ref[...] = jnp.where(even, mine, theirs) + mul_nt(jnp.where(even, theirs, mine), y)


def row_v_kernel(duo_v, other_v, partner_v, duo_y, other_y, partner_y, whole_ref, after_ref):
    x = x_of()
    low = x < 2
    mine, theirs, beside = duo_v[...], other_v[...], partner_v[:8]
    y = jnp.where(low, duo_y[:STATE], other_y[:STATE])
    whole_ref[...] = jnp.where(low, mine, theirs) + mul_nt(jnp.where(low, theirs, mine), y)
    outer = beside + mul_nt(theirs, partner_y[:STATE])
    after = jnp.where(x == 3, 0.0, jnp.where(x == 2, beside, theirs))
    after_ref[...] = jnp.where(x == 0, outer, after)


def leave_kernel(v1, v2, v3, near, far, side_ref, after_ref, *refs):
    out_ref = refs[-1]
    inner = v2[...] + mul_nt(v3[...], far[:STATE])
    sigma = v1[...] + mul_nt(inner, near[:STATE])
    out_ref[...] = mul_nt(sigma, side_ref[:STATE]) + after_ref[...]


def smooth_kernel(sigma_ref, sent_ref, other_ref, mid_ref, shi_ref, slo_ref, *refs):
    vecs = refs[:CHUNKS]
    m_ref, h_ref, smooth_ref = refs[CHUNKS:]
    crossed = mul_nt(sent_ref[...], other_ref[PART_Y : PART_Y + STATE]) + mid_ref[...]
    sigma = jnp.where(core_of() == 0, crossed, sigma_ref[...])
    gain = own_columns(jnp.concatenate([v[2] for v in vecs], axis=0))
    smooth_ref[...] = m_ref[...] + gain * (h_ref[...] + by_steps(sigma, shi_ref, slo_ref))


def over_z(a, s):
    return lax.ppermute(a, "state", [(i, (i + s) % 4) for i in range(4)])


def chip(x, y, c):
    return (y * 4 + x) * 2 + c


def over_core(a):
    return lax.ppermute(a, "tm", [(i, i ^ 1) for i in range(32)])


def over_x(a, to, pairs=((0, 0), (1, 1))):
    route = [
        (chip(x, y, c), chip(to(x), y, d)) for y in range(4) for x in range(4) for c, d in pairs
    ]
    return lax.ppermute(a, "tm", route)


def beside(x):
    return x ^ 1


def opposite(x):
    return 3 - x


def over_y(a, up=(), down=()):
    route = [(chip(x, a, 0), chip(x, b, 0)) for a, b in up for x in range(4)]
    route += [(chip(x, a, 1), chip(x, b, 1)) for a, b in down for x in range(4)]
    return lax.ppermute(a, "tm", route)


def gather_z(chunks):
    ahead = [over_z(a, 1) for a in chunks]
    behind = [over_z(a, 3) for a in chunks]
    return [
        [a, ahead[q], over_z(ahead[q] if RELAYS[q] == 1 else behind[q], RELAYS[q]), behind[q]]
        for q, a in enumerate(chunks)
    ]


def shards(dynamics, band, observed, obs_mask, filter_gain, smooth_gain):
    packed = call(
        pack_kernel,
        0,
        [arr(PER_STEP * size, 128) for size in SIZES],
        [dynamics, band.transpose(1, 2, 0).reshape(2, STEPS), observed, obs_mask, filter_gain, smooth_gain],
        [
            pltpu.VMEM((STEPS, 3 * BLOCK * BLOCK), f32),
            pltpu.VMEM((2, STEPS), jnp.int32),
            pltpu.VMEM((STEPS, BLOCK), f32),
            pltpu.VMEM((STEPS, BLOCK), jnp.int32),
            pltpu.VMEM((STEPS, BLOCK), f32),
            pltpu.VMEM((STEPS, BLOCK), f32),
            pltpu.SemaphoreType.DMA((6,)),
        ],
        raw=True,
        limit=60,
    )
    his, los, this, tlos, vecs, state = [], [], [], [], [], []
    for q, parts in enumerate(gather_z(packed)):
        size = SIZES[q]
        kept = call(
            functools.partial(chunk_kernel, q == 0, size),
            0.4 * size,
            [arr(size, STATE, STATE, dtype=bf16)] * 4 + [arr(4, size, STATE), arr(ROWS, STATE)],
            parts + state,
        )
        for store, value in zip((his, los, this, tlos, vecs), kept):
            store.append(value)
        own = kept[-1]
        state = [own]
    other = over_core(own)
    (side_own,) = call(pair_kernel, 0, [arr(AUG, STATE)], [own, other])
    partner = over_x(side_own, beside)
    zhi, zlo, thi, tlo, v_all, z_own = call(
        suffix_z_kernel,
        0,
        [arr(STEPS // 4, STATE, STATE, dtype=bf16)] * 4 + [arr(STEPS, STATE), arr(AUG, STATE)],
        his + los + this + tlos + vecs,
    )
    (duo,) = call(duo_kernel, 0, [arr(AUG, STATE)], [side_own, partner, z_own])
    other_duo = over_x(duo, opposite)
    z_other = over_core(z_own)
    shi, slo = call(
        suffix_kernel, 0, [arr(STEPS // 4, STATE, STATE, dtype=bf16)] * 2, his + los + vecs
    )
    whole, side, tail = call(
        row_kernel,
        0,
        [arr(AUG, STATE)] * 2 + [arr(8, STATE)],
        [partner, duo, other_duo, z_other, shi],
    )
    tail = over_y(tail, ((0, 3),))
    near = over_y(whole, ((0, 1), (1, 2), (2, 3)), ((2, 1), (1, 0)))
    far = over_y(whole, ((0, 2), (1, 3)), ((2, 0),))
    (z_chip,) = call(pair_z_kernel, 0, [arr(AUG, STATE)], [own, other, z_own, z_other])
    means, v_chip = call(
        enter_kernel,
        0,
        [arr(24, STATE), arr(48, STATE)],
        [near, far, tail, side, own, z_chip],
    )
    partner_v = over_x(v_chip, beside, ((0, 1),))
    sent = over_core(means)
    filtered, h_all, mid = call(
        local_kernel,
        0,
        [arr(STEPS, BLOCK)] * 2 + [arr(8, STATE)],
        [means, sent, z_other, zhi, zlo, thi, tlo, v_all] + vecs,
    )
    (duo_v,) = call(
        duo_v_kernel, 0, [arr(8, STATE)], [sent, partner_v, side_own, partner, h_all]
    )
    other_v = over_x(duo_v, opposite, ((1, 1),))
    v_row, v_after = call(
        row_v_kernel,
        0,
        [arr(8, STATE)] * 2,
        [duo_v, other_v, partner_v, duo, other_duo, partner],
    )
    v_rows = [
        over_y(v_row, (), ((3, 2), (2, 1), (1, 0))),
        over_y(v_row, (), ((3, 1), (2, 0))),
        over_y(v_row, (), ((3, 0),)),
    ]
    (sigma,) = call(leave_kernel, 0, [arr(8, STATE)], v_rows + [near, far, side, v_after])
    crossed = over_core(sigma)
    (smoothed,) = call(
        smooth_kernel,
        0,
        [arr(STEPS, BLOCK)],
        [sigma, crossed, other, mid, shi, slo] + vecs + [filtered, h_all],
    )
    return filtered, smoothed


def solution(mesh):
    in_specs = (
        P("tm", "state"),
        P("tm", "state", None),
        P("tm", "state"),
        P("tm", "state"),
        P("tm", "state"),
        P("tm", "state"),
    )
    out_specs = (P("tm", "state"), P("tm", "state"))
    return jax.shard_map(shards, mesh=mesh, in_specs=in_specs, out_specs=out_specs, check_vma=False)
```

```python
import functools

import jax
import jax.numpy as jnp
from jax import lax
from jax.experimental import pallas as pl
from jax.experimental.pallas import tpu as pltpu
from jax.sharding import PartitionSpec as P

BLOCK = 64
STATE = 256
BLOCKS = 4
STEPS = 16
SIZES = (4, 4, 4, 4)
RELAYS = (1, 1, 3, 3)
CHUNKS = len(SIZES)
STARTS = tuple(sum(SIZES[:q]) for q in range(CHUNKS))
AUG = STATE + 8
MIB = 1 << 20

f32 = jnp.float32
bf16 = jnp.bfloat16


def split(a):
    hi = a.astype(bf16)
    return hi, (a - hi.astype(f32)).astype(bf16)


def dot_nn(a, b):
    return lax.dot_general(a, b, (((1,), (0,)), ((), ())), preferred_element_type=f32)


def dot_nt(a, b):
    return lax.dot_general(a, b, (((1,), (1,)), ((), ())), preferred_element_type=f32)


def three(dot, a, b):
    ahi, alo = a
    bhi, blo = b
    return dot(ahi, bhi) + (dot(alo, bhi) + dot(ahi, blo))


def rows_by(dot, a, b):
    high = a.astype(bf16).astype(f32)
    both = jnp.concatenate([high, a - high], axis=0).astype(bf16)
    wide = dot(both, b[0]) + dot(both, b[1])
    return wide[:8] + wide[8:]


def mul_by(dot, a, b):
    if a.shape[0] == 8:
        return rows_by(dot, a, split(b))
    return three(dot, split(a), split(b))


def mul_nn(a, b):
    return mul_by(dot_nn, a, b)


def mul_nt(a, b):
    return mul_by(dot_nt, a, b)


def first_row(row):
    spread = jnp.broadcast_to(row, (8, row.shape[1]))
    return jnp.where(lax.broadcasted_iota(jnp.int32, spread.shape, 0) == 0, spread, 0.0)


def identity_matrix():
    rows = lax.broadcasted_iota(jnp.int32, (STATE, STATE), 0)
    cols = lax.broadcasted_iota(jnp.int32, (STATE, STATE), 1)
    return jnp.where(rows == cols, 1.0, 0.0).astype(f32)


def call(kernel, us, outs, args, scratch=(), raw=False, limit=40):
    vmem = pl.BlockSpec(memory_space=pltpu.VMEM)
    moved = sum(a.size * a.dtype.itemsize for a in args) + sum(
        o.size * o.dtype.itemsize for o in outs
    )
    return pl.pallas_call(
        kernel,
        out_shape=outs,
        in_specs=[pl.BlockSpec(memory_space=pltpu.HBM) if raw else vmem] * len(args),
        out_specs=[vmem] * len(outs),
        scratch_shapes=list(scratch),
        compiler_params=pltpu.CompilerParams(vmem_limit_bytes=limit * MIB),
        cost_estimate=pl.CostEstimate(flops=int(us * 1e9), bytes_accessed=moved, transcendentals=0),
    )(*args)


def arr(*shape, dtype=f32):
    return jax.ShapeDtypeStruct(shape, dtype)


def core_of():
    return lax.rem(lax.axis_index("tm"), 2)


def x_of():
    return lax.rem(lax.axis_index("tm") // 2, 4)


def y_of():
    return lax.axis_index("tm") // 8


PER_STEP = BLOCK + BLOCK // 2 + 2
PART_Y = AUG
ROWS = 2 * AUG
ENDS = tuple((q, i) for q in range(CHUNKS) for i in range(SIZES[q]))


def pack_kernel(dyn_hbm, band_hbm, obs_hbm, mask_hbm, fgain_hbm, sgain_hbm, *refs):
    outs = refs[:CHUNKS]
    dyn_ref, band_ref, obs_ref, mask_ref, fgain_ref, sgain_ref, sems = refs[CHUNKS:]
    copies = [
        pltpu.make_async_copy(src, dst, sems.at[i])
        for i, (src, dst) in enumerate(
            (
                (dyn_hbm, dyn_ref),
                (band_hbm, band_ref),
                (obs_hbm, obs_ref),
                (mask_hbm, mask_ref),
                (fgain_hbm, fgain_ref),
                (sgain_hbm, sgain_ref),
            )
        )
    ]
    for copy in copies:
        copy.start()
    for copy in copies:
        copy.wait()
    place = lax.axis_index("state")
    row = lax.broadcasted_iota(jnp.int32, (2, STEPS), 0)
    outside = jnp.where(place == 0, 0, jnp.where(place == BLOCKS - 1, 1, 2))
    band = jnp.where(row == outside, 0, band_ref[...]).astype(f32)
    band = jnp.transpose(jnp.concatenate([band, jnp.zeros((6, STEPS), f32)], axis=0))
    lower, upper = band[:, 0:1], band[:, 1:2]
    half = BLOCK // 2
    wide = 3 * BLOCK

    def put(at, value):
        for t0, size, out in zip(STARTS, SIZES, outs):
            out[at * size : (at + 1) * size, :] = value[t0 : t0 + size]

    for r in range(BLOCK):
        before = dyn_ref[:, r * wide : r * wide + BLOCK] * lower
        own = dyn_ref[:, r * wide + BLOCK : r * wide + 2 * BLOCK]
        put(r, jnp.concatenate([before, own], axis=1))
    for r in range(half):
        s = r + half
        near = dyn_ref[:, r * wide + 2 * BLOCK : (r + 1) * wide] * upper
        far = dyn_ref[:, s * wide + 2 * BLOCK : (s + 1) * wide] * upper
        put(BLOCK + r, jnp.concatenate([near, far], axis=1))
    weight = mask_ref[...].astype(f32) * fgain_ref[...]
    gain = sgain_ref[...]
    put(BLOCK + half, jnp.concatenate([weight, obs_ref[...]], axis=1))
    put(BLOCK + half + 1, jnp.concatenate([gain, gain], axis=1))


def chunk_kernel(first, size, *refs):
    parts = refs[:BLOCKS]
    state_ref, fhi_ref, flo_ref, thi_ref, tlo_ref, vec_ref, out_ref = (
        (None,) if first else ()
    ) + refs[BLOCKS:]
    place = lax.axis_index("state")
    zeros64 = jnp.zeros((BLOCK, BLOCK), f32)
    zero = jnp.zeros((size, STATE - BLOCK), f32)
    vecs = [None] * 3
    pairs_at = BLOCK * size
    vecs_at = pairs_at + BLOCK // 2 * size
    for s, m in enumerate(parts):
        block = lax.rem(place - s + BLOCKS, BLOCKS)
        shift = lax.rem(block + BLOCKS - 1, BLOCKS) * BLOCK
        rows = pl.ds(pl.multiple_of(block * BLOCK, BLOCK), BLOCK)
        for t in range(size):
            left = m[pl.ds(t, BLOCK, stride=size), :]
            pair = m[pl.ds(pairs_at + t, BLOCK // 2, stride=size), :]
            after = jnp.concatenate([pair[:, :BLOCK], pair[:, BLOCK:]], axis=0)
            full = jnp.concatenate([left, after, zeros64], axis=1)
            hi, lo = split(pltpu.roll(full, shift, 1))
            fhi_ref[t, rows, :] = hi
            flo_ref[t, rows, :] = lo
        wo = m[vecs_at : vecs_at + size, :]
        g = m[vecs_at + size : vecs_at + 2 * size, :]
        for i, piece in enumerate((wo[:, :BLOCK], wo[:, BLOCK:], g[:, :BLOCK])):
            piece = pltpu.roll(jnp.concatenate([piece, zero], axis=1), block * BLOCK, 1)
            vecs[i] = piece if vecs[i] is None else vecs[i] + piece
    for i in range(3):
        vec_ref[i] = vecs[i]
    if first:
        x = jnp.concatenate([identity_matrix(), jnp.zeros((8, STATE), f32)], axis=0)
        y = identity_matrix()
    else:
        x = state_ref[:AUG]
        y = state_ref[PART_Y : PART_Y + STATE]
    for t in range(size):
        w, o, g = (vecs[i][t : t + 1, :] for i in range(3))
        step = (fhi_ref[t], flo_ref[t])
        moved = three(dot_nt, split(x), step)
        thi_ref[t], tlo_ref[t] = split(moved[:STATE])
        vec_ref[3, t : t + 1, :] = moved[STATE : STATE + 1]
        kept = moved * (1.0 - w)
        x = jnp.concatenate([kept[:STATE], kept[STATE:] + first_row(w * o)], axis=0)
        y = three(dot_nt, split(y), step) * g
    out_ref[:AUG] = x
    out_ref[PART_Y : PART_Y + STATE] = y
    out_ref[PART_Y + STATE :] = jnp.zeros((8, STATE), f32)


def then(first, second):
    both = mul_nn(first, second[:STATE])
    return jnp.concatenate([both[:STATE], both[STATE:] + second[STATE:]], axis=0)


def pair_kernel(own_ref, other_ref, out_ref):
    core = core_of()
    part = pl.ds(pl.multiple_of(core * AUG, 8), AUG)
    own, other = own_ref[part, :], other_ref[part, :]
    lead = core == 0
    out_ref[...] = then(jnp.where(lead, own, other), jnp.where(lead, other, own))


def pair_z_kernel(own_ref, other_ref, z_own, z_other, z_ref):
    lead = core_of() == 0
    xl = jnp.where(lead, own_ref[:AUG], other_ref[:AUG])
    yl = jnp.where(lead, own_ref[PART_Y : PART_Y + STATE], other_ref[PART_Y : PART_Y + STATE])
    zl = jnp.where(lead, z_own[...], z_other[...])
    zr = jnp.where(lead, z_other[...], z_own[...])
    z_ref[...] = zl + mul_nt(then(xl, zr), yl)


def own_columns(a):
    place = lax.axis_index("state")
    own = a[:, :BLOCK]
    for b in range(1, BLOCKS):
        own = jnp.where(place == b, a[:, b * BLOCK : (b + 1) * BLOCK], own)
    return own


def own_pair(first, second):
    place = lax.axis_index("state")
    two = 2 * BLOCK
    odd = lax.rem(place, 2) == 1
    first, second = (
        jnp.where(place < 2, a[:, :two], a[:, two:]) for a in (first, second)
    )
    low = jnp.where(odd, pltpu.roll(first, BLOCK, 1), first)
    high = jnp.where(odd, second, pltpu.roll(second, BLOCK, 1))
    lane = lax.broadcasted_iota(jnp.int32, low.shape, 1)
    return jnp.where(lane < BLOCK, low, high)


def put_pair(hi_ref, lo_ref, slot, first, second):
    at = slot % 4 * BLOCK
    part = slice(at, at + 2 * BLOCK)
    hi_ref[slot // 4, :, part], lo_ref[slot // 4, :, part] = split(own_pair(first, second))


def by_steps(row, hi_ref, lo_ref):
    rows = []
    for k in range(STEPS // 4):
        wide = rows_by(dot_nn, row, (hi_ref[k], lo_ref[k]))[0:1]
        rows += [wide[:, i * BLOCK : (i + 1) * BLOCK] for i in range(4)]
    return jnp.concatenate(rows, axis=0)


def suffix_kernel(*refs):
    his, los, vecs = (refs[i * CHUNKS : (i + 1) * CHUNKS] for i in range(3))
    shi_ref, slo_ref = refs[-2:]
    run = held = identity_matrix()
    for t in range(STEPS - 1, 0, -1):
        q, i = ENDS[t]
        run = three(dot_nn, split(run * vecs[q][2, i : i + 1, :]), (his[q][i], los[q][i]))
        if t % 2 == 0:
            held = run
        else:
            put_pair(shi_ref, slo_ref, t - 1, run, held)


def suffix_z_kernel(*refs):
    his, los, this, tlos, vecs = (refs[i * CHUNKS : (i + 1) * CHUNKS] for i in range(5))
    zhi_ref, zlo_ref, thi_ref, tlo_ref, v_ref, z_ref = refs[5 * CHUNKS :]
    z = held = jnp.zeros((STATE, STATE), f32)
    v = jnp.zeros((8, STATE), f32)
    v_ref[...] = jnp.zeros((STEPS, STATE), f32)
    for t in range(STEPS - 1, -1, -1):
        q, i = ENDS[t]
        w, o, g, p = (vecs[q][k, i : i + 1, :] for k in range(4))
        step = (his[q][i], los[q][i])
        moved = this[q][i].astype(f32) + tlos[q][i].astype(f32)
        if t % 2 == 0:
            put_pair(thi_ref, tlo_ref, t, moved, after)
        after = moved
        z = three(dot_nn, split(z * g - moved * w), step)
        v = rows_by(dot_nn, v * g + first_row(w * (o - p)), step)
        if t > 0:
            v_ref[t - 1 : t, :] = v[0:1]
            if t % 2 == 0:
                held = z
            else:
                put_pair(zhi_ref, zlo_ref, t - 1, z, held)
    z_ref[:STATE] = z
    z_ref[STATE:] = v


def duo_kernel(own, partner, _, out_ref):
    even = lax.rem(x_of(), 2) == 0
    mine, theirs = own[...], partner[...]
    out_ref[...] = then(jnp.where(even, mine, theirs), jnp.where(even, theirs, mine))


def row_kernel(partner, duo, other_duo, *refs):
    whole_ref, side_ref, tail_ref, wide_ref = refs[-4:]
    x = x_of()
    lead = core_of() == 0
    low = x < 2
    mine, theirs, beside = duo[...], other_duo[...], partner[...]
    whole = then(jnp.where(low, mine, theirs), jnp.where(low, theirs, mine))
    whole_ref[...] = whole
    wide_ref[:AUG] = whole
    wide_ref[AUG:] = jnp.zeros((8, STATE), f32)
    tail_ref[:8] = whole[STATE:]
    outer = then(jnp.where(lead, theirs, beside), jnp.where(lead, beside, theirs))
    nothing = jnp.concatenate([identity_matrix(), jnp.zeros((8, STATE), f32)], axis=0)
    depth = jnp.where(lead, x, 3 - x)
    side = jnp.where(depth == 0, nothing, jnp.where(depth == 1, beside, theirs))
    side_ref[...] = jnp.where(depth == 3, outer, side)


def enter_kernel(near, far, tail2, tail3, side_ref, own_ref, z_chip, means_ref, v_ref):
    y = y_of()
    through = mul_nn(tail3[...], far[:STATE]) + far[STATE:]
    inner = jnp.where(y == 3, through, tail2[...])
    m = mul_nn(inner, near[:STATE]) + near[STATE:AUG]
    m = mul_nn(m, side_ref[:STATE]) + side_ref[STATE:]
    v = mul_nn(m, z_chip[:STATE]) + z_chip[STATE:]
    v_ref[:8] = v
    v_ref[8:] = jnp.zeros((40, STATE), f32)
    means_ref[:8] = v
    means_ref[8:16] = m
    means_ref[16:] = mul_nn(m, own_ref[:STATE]) + own_ref[STATE:AUG]


def local_kernel(
    means_ref, sent_ref, z_other, zhi_ref, zlo_ref, thi_ref, tlo_ref, v_ref, *refs
):
    vecs = refs[:CHUNKS]
    m_ref, h_ref, mid_ref = refs[CHUNKS:]
    mid_ref[...] = mul_nn(means_ref[16:], z_other[:STATE]) + z_other[STATE:]
    enter = jnp.where(core_of() == 0, means_ref[8:16], sent_ref[16:])
    w, o, p = (
        own_columns(jnp.concatenate([v[k] for v in vecs], axis=0)) for k in (0, 1, 3)
    )
    p = by_steps(enter, thi_ref, tlo_ref) + p
    m_ref[...] = p + w * (o - p)
    h_ref[...] = by_steps(enter, zhi_ref, zlo_ref) + own_columns(v_ref[...])


def duo_v_kernel(sent, partner_v, own_y, partner_y, _, out_ref):
    even = lax.rem(x_of(), 2) == 0
    mine, theirs = sent[:8], partner_v[:8]
    y = jnp.where(even, own_y[:STATE], partner_y[:STATE])
    out_ref[...] = jnp.where(even, mine, theirs) + mul_nt(jnp.where(even, theirs, mine), y)


def row_v_kernel(duo_v, other_v, partner_v, duo_y, other_y, partner_y, whole_ref, after_ref):
    x = x_of()
    low = x < 2
    mine, theirs, beside = duo_v[...], other_v[...], partner_v[:8]
    y = jnp.where(low, duo_y[:STATE], other_y[:STATE])
    whole_ref[...] = jnp.where(low, mine, theirs) + mul_nt(jnp.where(low, theirs, mine), y)
    outer = beside + mul_nt(theirs, partner_y[:STATE])
    after = jnp.where(x == 3, 0.0, jnp.where(x == 2, beside, theirs))
    after_ref[...] = jnp.where(x == 0, outer, after)


def leave_kernel(v1, v2, v3, near, far, side_ref, after_ref, *refs):
    out_ref = refs[-1]
    inner = v2[...] + mul_nt(v3[...], far[:STATE])
    sigma = v1[...] + mul_nt(inner, near[:STATE])
    out_ref[...] = mul_nt(sigma, side_ref[:STATE]) + after_ref[...]


def smooth_kernel(sigma_ref, sent_ref, other_ref, mid_ref, shi_ref, slo_ref, *refs):
    vecs = refs[:CHUNKS]
    m_ref, h_ref, smooth_ref = refs[CHUNKS:]
    crossed = mul_nt(sent_ref[...], other_ref[PART_Y : PART_Y + STATE]) + mid_ref[...]
    sigma = jnp.where(core_of() == 0, crossed, sigma_ref[...])
    gain = own_columns(jnp.concatenate([v[2] for v in vecs], axis=0))
    smooth_ref[...] = m_ref[...] + gain * (h_ref[...] + by_steps(sigma, shi_ref, slo_ref))


def over_z(a, s):
    return lax.ppermute(a, "state", [(i, (i + s) % 4) for i in range(4)])


def chip(x, y, c):
    return (y * 4 + x) * 2 + c


def over_core(a):
    return lax.ppermute(a, "tm", [(i, i ^ 1) for i in range(32)])


def over_x(a, to, pairs=((0, 0), (1, 1))):
    route = [
        (chip(x, y, c), chip(to(x), y, d)) for y in range(4) for x in range(4) for c, d in pairs
    ]
    return lax.ppermute(a, "tm", route)


def beside(x):
    return x ^ 1


def opposite(x):
    return 3 - x


def over_y(a, up=(), down=()):
    route = [(chip(x, a, 0), chip(x, b, 0)) for a, b in up for x in range(4)]
    route += [(chip(x, a, 1), chip(x, b, 1)) for a, b in down for x in range(4)]
    return lax.ppermute(a, "tm", route)


def gather_z(chunks):
    ahead = [over_z(a, 1) for a in chunks]
    behind = [over_z(a, 3) for a in chunks]
    return [
        [a, ahead[q], over_z(ahead[q] if RELAYS[q] == 1 else behind[q], RELAYS[q]), behind[q]]
        for q, a in enumerate(chunks)
    ]


def shards(dynamics, band, observed, obs_mask, filter_gain, smooth_gain):
    packed = call(
        pack_kernel,
        0,
        [arr(PER_STEP * size, 128) for size in SIZES],
        [dynamics, band.transpose(1, 2, 0).reshape(2, STEPS), observed, obs_mask, filter_gain, smooth_gain],
        [
            pltpu.VMEM((STEPS, 3 * BLOCK * BLOCK), f32),
            pltpu.VMEM((2, STEPS), jnp.int32),
            pltpu.VMEM((STEPS, BLOCK), f32),
            pltpu.VMEM((STEPS, BLOCK), jnp.int32),
            pltpu.VMEM((STEPS, BLOCK), f32),
            pltpu.VMEM((STEPS, BLOCK), f32),
            pltpu.SemaphoreType.DMA((6,)),
        ],
        raw=True,
        limit=60,
    )
    his, los, this, tlos, vecs, state = [], [], [], [], [], []
    for q, parts in enumerate(gather_z(packed)):
        size = SIZES[q]
        kept = call(
            functools.partial(chunk_kernel, q == 0, size),
            0.4 * size,
            [arr(size, STATE, STATE, dtype=bf16)] * 4 + [arr(4, size, STATE), arr(ROWS, STATE)],
            parts + state,
        )
        for store, value in zip((his, los, this, tlos, vecs), kept):
            store.append(value)
        own = kept[-1]
        state = [own]
    other = over_core(own)
    (side_own,) = call(pair_kernel, 0, [arr(AUG, STATE)], [own, other])
    partner = over_x(side_own, beside)
    zhi, zlo, thi, tlo, v_all, z_own = call(
        suffix_z_kernel,
        0,
        [arr(STEPS // 4, STATE, STATE, dtype=bf16)] * 4 + [arr(STEPS, STATE), arr(AUG, STATE)],
        his + los + this + tlos + vecs,
    )
    (duo,) = call(duo_kernel, 0, [arr(AUG, STATE)], [side_own, partner, z_own])
    other_duo = over_x(duo, opposite)
    z_other = over_core(z_own)
    shi, slo = call(
        suffix_kernel, 0, [arr(STEPS // 4, STATE, STATE, dtype=bf16)] * 2, his + los + vecs
    )
    whole, side, tail, wide = call(
        row_kernel,
        0,
        [arr(AUG, STATE)] * 2 + [arr(8, STATE), arr(AUG + 8, STATE)],
        [partner, duo, other_duo, z_other, shi],
    )
    tails = [over_y(tail, ((0, 2),)), over_y(tail, ((0, 3),))]
    near = over_y(wide, ((0, 1), (1, 2), (2, 3)), ((2, 1), (1, 0)))
    far = over_y(whole, ((1, 3),), ((2, 0),))
    (z_chip,) = call(pair_z_kernel, 0, [arr(AUG, STATE)], [own, other, z_own, z_other])
    means, v_chip = call(
        enter_kernel,
        0,
        [arr(24, STATE), arr(48, STATE)],
        [near, far] + tails + [side, own, z_chip],
    )
    partner_v = over_x(v_chip, beside, ((0, 1),))
    sent = over_core(means)
    filtered, h_all, mid = call(
        local_kernel,
        0,
        [arr(STEPS, BLOCK)] * 2 + [arr(8, STATE)],
        [means, sent, z_other, zhi, zlo, thi, tlo, v_all] + vecs,
    )
    (duo_v,) = call(
        duo_v_kernel, 0, [arr(8, STATE)], [sent, partner_v, side_own, partner, h_all]
    )
    other_v = over_x(duo_v, opposite, ((1, 1),))
    v_row, v_after = call(
        row_v_kernel,
        0,
        [arr(8, STATE)] * 2,
        [duo_v, other_v, partner_v, duo, other_duo, partner],
    )
    v_rows = [
        over_y(v_row, (), ((3, 2), (2, 1), (1, 0))),
        over_y(v_row, (), ((3, 1), (2, 0))),
        over_y(v_row, (), ((3, 0),)),
    ]
    (sigma,) = call(leave_kernel, 0, [arr(8, STATE)], v_rows + [near, far, side, v_after])
    crossed = over_core(sigma)
    (smoothed,) = call(
        smooth_kernel,
        0,
        [arr(STEPS, BLOCK)],
        [sigma, crossed, other, mid, shi, slo] + vecs + [filtered, h_all],
    )
    return filtered, smoothed


def solution(mesh):
    in_specs = (
        P("tm", "state"),
        P("tm", "state", None),
        P("tm", "state"),
        P("tm", "state"),
        P("tm", "state"),
        P("tm", "state"),
    )
    out_specs = (P("tm", "state"), P("tm", "state"))
    return jax.shard_map(shards, mesh=mesh, in_specs=in_specs, out_specs=out_specs, check_vma=False)
```

```python
import functools

import jax
import jax.numpy as jnp
from jax import lax
from jax.experimental import pallas as pl
from jax.experimental.pallas import tpu as pltpu
from jax.sharding import PartitionSpec as P

BLOCK = 64
STATE = 256
BLOCKS = 4
STEPS = 16
SIZES = (4, 4, 4, 4)
RELAYS = (1, 1, 3, 3)
CHUNKS = len(SIZES)
STARTS = tuple(sum(SIZES[:q]) for q in range(CHUNKS))
AUG = STATE + 8
MIB = 1 << 20

f32 = jnp.float32
bf16 = jnp.bfloat16


def split(a):
    hi = a.astype(bf16)
    return hi, (a - hi.astype(f32)).astype(bf16)


def dot_nn(a, b):
    return lax.dot_general(a, b, (((1,), (0,)), ((), ())), preferred_element_type=f32)


def dot_nt(a, b):
    return lax.dot_general(a, b, (((1,), (1,)), ((), ())), preferred_element_type=f32)


def three(dot, a, b):
    ahi, alo = a
    bhi, blo = b
    return dot(ahi, bhi) + (dot(alo, bhi) + dot(ahi, blo))


def rows_by(dot, a, b):
    high = a.astype(bf16).astype(f32)
    both = jnp.concatenate([high, a - high], axis=0).astype(bf16)
    wide = dot(both, b[0]) + dot(both, b[1])
    return wide[:8] + wide[8:]


def mul_by(dot, a, b):
    if a.shape[0] == 8:
        return rows_by(dot, a, split(b))
    return three(dot, split(a), split(b))


def mul_nn(a, b):
    return mul_by(dot_nn, a, b)


def mul_nt(a, b):
    return mul_by(dot_nt, a, b)


def first_row(row):
    spread = jnp.broadcast_to(row, (8, row.shape[1]))
    return jnp.where(lax.broadcasted_iota(jnp.int32, spread.shape, 0) == 0, spread, 0.0)


def identity_matrix():
    rows = lax.broadcasted_iota(jnp.int32, (STATE, STATE), 0)
    cols = lax.broadcasted_iota(jnp.int32, (STATE, STATE), 1)
    return jnp.where(rows == cols, 1.0, 0.0).astype(f32)


def call(kernel, us, outs, args, scratch=(), raw=False, limit=40):
    vmem = pl.BlockSpec(memory_space=pltpu.VMEM)
    moved = sum(a.size * a.dtype.itemsize for a in args) + sum(
        o.size * o.dtype.itemsize for o in outs
    )
    return pl.pallas_call(
        kernel,
        out_shape=outs,
        in_specs=[pl.BlockSpec(memory_space=pltpu.HBM) if raw else vmem] * len(args),
        out_specs=[vmem] * len(outs),
        scratch_shapes=list(scratch),
        compiler_params=pltpu.CompilerParams(vmem_limit_bytes=limit * MIB),
        cost_estimate=pl.CostEstimate(flops=int(us * 1e9), bytes_accessed=moved, transcendentals=0),
    )(*args)


def arr(*shape, dtype=f32):
    return jax.ShapeDtypeStruct(shape, dtype)


def core_of():
    return lax.rem(lax.axis_index("tm"), 2)


def x_of():
    return lax.rem(lax.axis_index("tm") // 2, 4)


def y_of():
    return lax.axis_index("tm") // 8


PER_STEP = BLOCK + BLOCK // 2 + 2
PART_Y = AUG
ROWS = 2 * AUG
ENDS = tuple((q, i) for q in range(CHUNKS) for i in range(SIZES[q]))


def pack_kernel(dyn_hbm, band_hbm, obs_hbm, mask_hbm, fgain_hbm, sgain_hbm, *refs):
    outs = refs[:CHUNKS]
    dyn_ref, band_ref, obs_ref, mask_ref, fgain_ref, sgain_ref, sems = refs[CHUNKS:]
    copies = [
        pltpu.make_async_copy(src, dst, sems.at[i])
        for i, (src, dst) in enumerate(
            (
                (dyn_hbm, dyn_ref),
                (band_hbm, band_ref),
                (obs_hbm, obs_ref),
                (mask_hbm, mask_ref),
                (fgain_hbm, fgain_ref),
                (sgain_hbm, sgain_ref),
            )
        )
    ]
    for copy in copies:
        copy.start()
    for copy in copies:
        copy.wait()
    place = lax.axis_index("state")
    row = lax.broadcasted_iota(jnp.int32, (2, STEPS), 0)
    outside = jnp.where(place == 0, 0, jnp.where(place == BLOCKS - 1, 1, 2))
    band = jnp.where(row == outside, 0, band_ref[...]).astype(f32)
    band = jnp.transpose(jnp.concatenate([band, jnp.zeros((6, STEPS), f32)], axis=0))
    lower, upper = band[:, 0:1], band[:, 1:2]
    half = BLOCK // 2
    wide = 3 * BLOCK

    def put(at, value):
        for t0, size, out in zip(STARTS, SIZES, outs):
            out[at * size : (at + 1) * size, :] = value[t0 : t0 + size]

    for r in range(BLOCK):
        before = dyn_ref[:, r * wide : r * wide + BLOCK] * lower
        own = dyn_ref[:, r * wide + BLOCK : r * wide + 2 * BLOCK]
        put(r, jnp.concatenate([before, own], axis=1))
    for r in range(half):
        s = r + half
        near = dyn_ref[:, r * wide + 2 * BLOCK : (r + 1) * wide] * upper
        far = dyn_ref[:, s * wide + 2 * BLOCK : (s + 1) * wide] * upper
        put(BLOCK + r, jnp.concatenate([near, far], axis=1))
    weight = mask_ref[...].astype(f32) * fgain_ref[...]
    gain = sgain_ref[...]
    put(BLOCK + half, jnp.concatenate([weight, obs_ref[...]], axis=1))
    put(BLOCK + half + 1, jnp.concatenate([gain, gain], axis=1))


def chunk_kernel(first, size, *refs):
    parts = refs[:BLOCKS]
    state_ref, fhi_ref, flo_ref, thi_ref, tlo_ref, vec_ref, out_ref = (
        (None,) if first else ()
    ) + refs[BLOCKS:]
    place = lax.axis_index("state")
    zeros64 = jnp.zeros((BLOCK, BLOCK), f32)
    zero = jnp.zeros((size, STATE - BLOCK), f32)
    vecs = [None] * 3
    pairs_at = BLOCK * size
    vecs_at = pairs_at + BLOCK // 2 * size
    for s, m in enumerate(parts):
        block = lax.rem(place - s + BLOCKS, BLOCKS)
        shift = lax.rem(block + BLOCKS - 1, BLOCKS) * BLOCK
        rows = pl.ds(pl.multiple_of(block * BLOCK, BLOCK), BLOCK)
        for t in range(size):
            left = m[pl.ds(t, BLOCK, stride=size), :]
            pair = m[pl.ds(pairs_at + t, BLOCK // 2, stride=size), :]
            after = jnp.concatenate([pair[:, :BLOCK], pair[:, BLOCK:]], axis=0)
            full = jnp.concatenate([left, after, zeros64], axis=1)
            hi, lo = split(pltpu.roll(full, shift, 1))
            fhi_ref[t, rows, :] = hi
            flo_ref[t, rows, :] = lo
        wo = m[vecs_at : vecs_at + size, :]
        g = m[vecs_at + size : vecs_at + 2 * size, :]
        for i, piece in enumerate((wo[:, :BLOCK], wo[:, BLOCK:], g[:, :BLOCK])):
            piece = pltpu.roll(jnp.concatenate([piece, zero], axis=1), block * BLOCK, 1)
            vecs[i] = piece if vecs[i] is None else vecs[i] + piece
    for i in range(3):
        vec_ref[i] = vecs[i]
    if first:
        x = jnp.concatenate([identity_matrix(), jnp.zeros((8, STATE), f32)], axis=0)
        y = identity_matrix()
    else:
        x = state_ref[:AUG]
        y = state_ref[PART_Y : PART_Y + STATE]
    for t in range(size):
        w, o, g = (vecs[i][t : t + 1, :] for i in range(3))
        step = (fhi_ref[t], flo_ref[t])
        moved = three(dot_nt, split(x), step)
        thi_ref[t], tlo_ref[t] = split(moved[:STATE])
        vec_ref[3, t : t + 1, :] = moved[STATE : STATE + 1]
        kept = moved * (1.0 - w)
        x = jnp.concatenate([kept[:STATE], kept[STATE:] + first_row(w * o)], axis=0)
        y = three(dot_nt, split(y), step) * g
    out_ref[:AUG] = x
    out_ref[PART_Y : PART_Y + STATE] = y
    out_ref[PART_Y + STATE :] = jnp.zeros((8, STATE), f32)


def then(first, second):
    both = mul_nn(first, second[:STATE])
    return jnp.concatenate([both[:STATE], both[STATE:] + second[STATE:]], axis=0)


def pair_kernel(own_ref, other_ref, out_ref):
    core = core_of()
    part = pl.ds(pl.multiple_of(core * AUG, 8), AUG)
    own, other = own_ref[part, :], other_ref[part, :]
    lead = core == 0
    out_ref[...] = then(jnp.where(lead, own, other), jnp.where(lead, other, own))


def pair_z_kernel(own_ref, other_ref, z_own, z_other, z_ref):
    lead = core_of() == 0
    xl = jnp.where(lead, own_ref[:AUG], other_ref[:AUG])
    yl = jnp.where(lead, own_ref[PART_Y : PART_Y + STATE], other_ref[PART_Y : PART_Y + STATE])
    zl = jnp.where(lead, z_own[...], z_other[...])
    zr = jnp.where(lead, z_other[...], z_own[...])
    z_ref[...] = zl + mul_nt(then(xl, zr), yl)


def own_columns(a):
    place = lax.axis_index("state")
    own = a[:, :BLOCK]
    for b in range(1, BLOCKS):
        own = jnp.where(place == b, a[:, b * BLOCK : (b + 1) * BLOCK], own)
    return own


def own_pair(first, second):
    place = lax.axis_index("state")
    two = 2 * BLOCK
    odd = lax.rem(place, 2) == 1
    first, second = (
        jnp.where(place < 2, a[:, :two], a[:, two:]) for a in (first, second)
    )
    low = jnp.where(odd, pltpu.roll(first, BLOCK, 1), first)
    high = jnp.where(odd, second, pltpu.roll(second, BLOCK, 1))
    lane = lax.broadcasted_iota(jnp.int32, low.shape, 1)
    return jnp.where(lane < BLOCK, low, high)


def put_pair(hi_ref, lo_ref, slot, first, second):
    at = slot % 4 * BLOCK
    part = slice(at, at + 2 * BLOCK)
    hi_ref[slot // 4, :, part], lo_ref[slot // 4, :, part] = split(own_pair(first, second))


def by_steps(row, hi_ref, lo_ref):
    rows = []
    for k in range(STEPS // 4):
        wide = rows_by(dot_nn, row, (hi_ref[k], lo_ref[k]))[0:1]
        rows += [wide[:, i * BLOCK : (i + 1) * BLOCK] for i in range(4)]
    return jnp.concatenate(rows, axis=0)


def suffix_kernel(*refs):
    his, los, vecs = (refs[i * CHUNKS : (i + 1) * CHUNKS] for i in range(3))
    shi_ref, slo_ref = refs[-2:]
    run = held = identity_matrix()
    for t in range(STEPS - 1, 0, -1):
        q, i = ENDS[t]
        run = three(dot_nn, split(run * vecs[q][2, i : i + 1, :]), (his[q][i], los[q][i]))
        if t % 2 == 0:
            held = run
        else:
            put_pair(shi_ref, slo_ref, t - 1, run, held)


def suffix_z_kernel(*refs):
    his, los, this, tlos, vecs = (refs[i * CHUNKS : (i + 1) * CHUNKS] for i in range(5))
    zhi_ref, zlo_ref, thi_ref, tlo_ref, v_ref, z_ref = refs[5 * CHUNKS :]
    z = held = jnp.zeros((STATE, STATE), f32)
    v = jnp.zeros((8, STATE), f32)
    v_ref[...] = jnp.zeros((STEPS, STATE), f32)
    for t in range(STEPS - 1, -1, -1):
        q, i = ENDS[t]
        w, o, g, p = (vecs[q][k, i : i + 1, :] for k in range(4))
        step = (his[q][i], los[q][i])
        moved = this[q][i].astype(f32) + tlos[q][i].astype(f32)
        if t % 2 == 0:
            put_pair(thi_ref, tlo_ref, t, moved, after)
        after = moved
        z = three(dot_nn, split(z * g - moved * w), step)
        v = rows_by(dot_nn, v * g + first_row(w * (o - p)), step)
        if t > 0:
            v_ref[t - 1 : t, :] = v[0:1]
            if t % 2 == 0:
                held = z
            else:
                put_pair(zhi_ref, zlo_ref, t - 1, z, held)
    z_ref[:STATE] = z
    z_ref[STATE:] = v


def duo_kernel(own, partner, _, out_ref):
    even = lax.rem(x_of(), 2) == 0
    mine, theirs = own[...], partner[...]
    out_ref[...] = then(jnp.where(even, mine, theirs), jnp.where(even, theirs, mine))


def row_kernel(partner, duo, other_duo, *refs):
    whole_ref, side_ref, tail_ref, wide_ref = refs[-4:]
    x = x_of()
    lead = core_of() == 0
    low = x < 2
    mine, theirs, beside = duo[...], other_duo[...], partner[...]
    whole = then(jnp.where(low, mine, theirs), jnp.where(low, theirs, mine))
    whole_ref[...] = whole
    wide_ref[:AUG] = whole
    wide_ref[AUG:] = jnp.zeros((8, STATE), f32)
    tail_ref[:8] = whole[STATE:]
    outer = then(jnp.where(lead, theirs, beside), jnp.where(lead, beside, theirs))
    nothing = jnp.concatenate([identity_matrix(), jnp.zeros((8, STATE), f32)], axis=0)
    depth = jnp.where(lead, x, 3 - x)
    side = jnp.where(depth == 0, nothing, jnp.where(depth == 1, beside, theirs))
    side_ref[...] = jnp.where(depth == 3, outer, side)


def enter_kernel(near, far, tail2, tail3, side_ref, z_chip, means_ref, v_ref):
    y = y_of()
    through = mul_nn(tail3[...], far[:STATE]) + far[STATE:]
    inner = jnp.where(y == 3, through, tail2[...])
    m = mul_nn(inner, near[:STATE]) + near[STATE:AUG]
    m = mul_nn(m, side_ref[:STATE]) + side_ref[STATE:]
    v = mul_nn(m, z_chip[:STATE]) + z_chip[STATE:]
    v_ref[:8] = v
    v_ref[8:] = jnp.zeros((40, STATE), f32)
    means_ref[:8] = v
    means_ref[8:] = m


def local_kernel(
    means_ref, sent_ref, x_own, x_other, z_other, zhi_ref, zlo_ref, thi_ref, tlo_ref, v_ref, *refs
):
    vecs = refs[:CHUNKS]
    m_ref, h_ref, mid_ref = refs[CHUNKS:]
    lead = core_of() == 0
    m = jnp.where(lead, means_ref[8:], sent_ref[8:])
    x = jnp.where(lead, x_own[:AUG], x_other[:AUG])
    mid = mul_nn(m, x[:STATE]) + x[STATE:]
    mid_ref[...] = mul_nn(mid, z_other[:STATE]) + z_other[STATE:]
    enter = jnp.where(lead, m, mid)
    w, o, p = (
        own_columns(jnp.concatenate([v[k] for v in vecs], axis=0)) for k in (0, 1, 3)
    )
    p = by_steps(enter, thi_ref, tlo_ref) + p
    m_ref[...] = p + w * (o - p)
    h_ref[...] = by_steps(enter, zhi_ref, zlo_ref) + own_columns(v_ref[...])


def duo_v_kernel(sent, partner_v, own_y, partner_y, _, out_ref):
    even = lax.rem(x_of(), 2) == 0
    mine, theirs = sent[:8], partner_v[:8]
    y = jnp.where(even, own_y[:STATE], partner_y[:STATE])
    out_ref[...] = jnp.where(even, mine, theirs) + mul_nt(jnp.where(even, theirs, mine), y)


def row_v_kernel(duo_v, other_v, partner_v, duo_y, other_y, partner_y, whole_ref, after_ref):
    x = x_of()
    low = x < 2
    mine, theirs, beside = duo_v[...], other_v[...], partner_v[:8]
    y = jnp.where(low, duo_y[:STATE], other_y[:STATE])
    whole_ref[...] = jnp.where(low, mine, theirs) + mul_nt(jnp.where(low, theirs, mine), y)
    outer = beside + mul_nt(theirs, partner_y[:STATE])
    after = jnp.where(x == 3, 0.0, jnp.where(x == 2, beside, theirs))
    after_ref[...] = jnp.where(x == 0, outer, after)


def leave_kernel(v1, v2, v3, near, far, side_ref, after_ref, *refs):
    out_ref = refs[-1]
    inner = v2[...] + mul_nt(v3[...], far[:STATE])
    sigma = v1[...] + mul_nt(inner, near[:STATE])
    out_ref[...] = mul_nt(sigma, side_ref[:STATE]) + after_ref[...]


def smooth_kernel(sigma_ref, sent_ref, other_ref, mid_ref, shi_ref, slo_ref, *refs):
    vecs = refs[:CHUNKS]
    m_ref, h_ref, smooth_ref = refs[CHUNKS:]
    crossed = mul_nt(sent_ref[...], other_ref[PART_Y : PART_Y + STATE]) + mid_ref[...]
    sigma = jnp.where(core_of() == 0, crossed, sigma_ref[...])
    gain = own_columns(jnp.concatenate([v[2] for v in vecs], axis=0))
    smooth_ref[...] = m_ref[...] + gain * (h_ref[...] + by_steps(sigma, shi_ref, slo_ref))


def over_z(a, s):
    return lax.ppermute(a, "state", [(i, (i + s) % 4) for i in range(4)])


def chip(x, y, c):
    return (y * 4 + x) * 2 + c


def over_core(a):
    return lax.ppermute(a, "tm", [(i, i ^ 1) for i in range(32)])


def over_x(a, to, pairs=((0, 0), (1, 1))):
    route = [
        (chip(x, y, c), chip(to(x), y, d)) for y in range(4) for x in range(4) for c, d in pairs
    ]
    return lax.ppermute(a, "tm", route)


def beside(x):
    return x ^ 1


def opposite(x):
    return 3 - x


def over_y(a, up=(), down=()):
    route = [(chip(x, a, 0), chip(x, b, 0)) for a, b in up for x in range(4)]
    route += [(chip(x, a, 1), chip(x, b, 1)) for a, b in down for x in range(4)]
    return lax.ppermute(a, "tm", route)


def gather_z(chunks):
    ahead = [over_z(a, 1) for a in chunks]
    behind = [over_z(a, 3) for a in chunks]
    return [
        [a, ahead[q], over_z(ahead[q] if RELAYS[q] == 1 else behind[q], RELAYS[q]), behind[q]]
        for q, a in enumerate(chunks)
    ]


def shards(dynamics, band, observed, obs_mask, filter_gain, smooth_gain):
    packed = call(
        pack_kernel,
        0,
        [arr(PER_STEP * size, 128) for size in SIZES],
        [dynamics, band.transpose(1, 2, 0).reshape(2, STEPS), observed, obs_mask, filter_gain, smooth_gain],
        [
            pltpu.VMEM((STEPS, 3 * BLOCK * BLOCK), f32),
            pltpu.VMEM((2, STEPS), jnp.int32),
            pltpu.VMEM((STEPS, BLOCK), f32),
            pltpu.VMEM((STEPS, BLOCK), jnp.int32),
            pltpu.VMEM((STEPS, BLOCK), f32),
            pltpu.VMEM((STEPS, BLOCK), f32),
            pltpu.SemaphoreType.DMA((6,)),
        ],
        raw=True,
        limit=60,
    )
    his, los, this, tlos, vecs, state = [], [], [], [], [], []
    for q, parts in enumerate(gather_z(packed)):
        size = SIZES[q]
        kept = call(
            functools.partial(chunk_kernel, q == 0, size),
            0.4 * size,
            [arr(size, STATE, STATE, dtype=bf16)] * 4 + [arr(4, size, STATE), arr(ROWS, STATE)],
            parts + state,
        )
        for store, value in zip((his, los, this, tlos, vecs), kept):
            store.append(value)
        own = kept[-1]
        state = [own]
    other = over_core(own)
    (side_own,) = call(pair_kernel, 0, [arr(AUG, STATE)], [own, other])
    partner = over_x(side_own, beside)
    zhi, zlo, thi, tlo, v_all, z_own = call(
        suffix_z_kernel,
        0,
        [arr(STEPS // 4, STATE, STATE, dtype=bf16)] * 4 + [arr(STEPS, STATE), arr(AUG, STATE)],
        his + los + this + tlos + vecs,
    )
    (duo,) = call(duo_kernel, 0, [arr(AUG, STATE)], [side_own, partner, z_own])
    other_duo = over_x(duo, opposite)
    z_other = over_core(z_own)
    shi, slo = call(
        suffix_kernel, 0, [arr(STEPS // 4, STATE, STATE, dtype=bf16)] * 2, his + los + vecs
    )
    whole, side, tail, wide = call(
        row_kernel,
        0,
        [arr(AUG, STATE)] * 2 + [arr(8, STATE), arr(AUG + 8, STATE)],
        [partner, duo, other_duo, z_other, shi],
    )
    tails = [over_y(tail, ((0, 2),)), over_y(tail, ((0, 3),))]
    near = over_y(wide, ((0, 1), (1, 2), (2, 3)), ((2, 1), (1, 0)))
    far = over_y(whole, ((1, 3),), ((2, 0),))
    (z_chip,) = call(pair_z_kernel, 0, [arr(AUG, STATE)], [own, other, z_own, z_other])
    means, v_chip = call(
        enter_kernel,
        0,
        [arr(16, STATE), arr(48, STATE)],
        [near, far] + tails + [side, z_chip],
    )
    partner_v = over_x(v_chip, beside, ((0, 1),))
    sent = over_core(means)
    filtered, h_all, mid = call(
        local_kernel,
        0,
        [arr(STEPS, BLOCK)] * 2 + [arr(8, STATE)],
        [means, sent, own, other, z_other, zhi, zlo, thi, tlo, v_all] + vecs,
    )
    (duo_v,) = call(
        duo_v_kernel, 0, [arr(8, STATE)], [sent, partner_v, side_own, partner, h_all]
    )
    other_v = over_x(duo_v, opposite, ((1, 1),))
    v_row, v_after = call(
        row_v_kernel,
        0,
        [arr(8, STATE)] * 2,
        [duo_v, other_v, partner_v, duo, other_duo, partner],
    )
    v_rows = [
        over_y(v_row, (), ((3, 2), (2, 1), (1, 0))),
        over_y(v_row, (), ((3, 1), (2, 0))),
        over_y(v_row, (), ((3, 0),)),
    ]
    (sigma,) = call(leave_kernel, 0, [arr(8, STATE)], v_rows + [near, far, side, v_after])
    crossed = over_core(sigma)
    (smoothed,) = call(
        smooth_kernel,
        0,
        [arr(STEPS, BLOCK)],
        [sigma, crossed, other, mid, shi, slo] + vecs + [filtered, h_all],
    )
    return filtered, smoothed


def solution(mesh):
    in_specs = (
        P("tm", "state"),
        P("tm", "state", None),
        P("tm", "state"),
        P("tm", "state"),
        P("tm", "state"),
        P("tm", "state"),
    )
    out_specs = (P("tm", "state"), P("tm", "state"))
    return jax.shard_map(shards, mesh=mesh, in_specs=in_specs, out_specs=out_specs, check_vma=False)
```
